256 devices in a mesh: row: 8 (over y, core), col: 32 (over x, z).
Axes of the slice: x: 4, y: 4, z: 8, core: 2. Of those that a mesh axis runs over, the one named last changes fastest.
Arguments:
- matrix: bfloat16 [8, 8, 256, 4, 32, 256], P(None, 'row', None, None, 'col'), as said below
- pattern: int32 [64, 128], replicated, may hold values from 0 to 1, as said below
- panel: int32 [1], replicated, may hold values from 0 to 47
Outputs:
- factored: float32 [8, 8, 256, 4, 32, 256], P(None, 'row', None, None, 'col')
The draws below stay inside these ranges and needn't reach their ends.
Inputs may be any that keep to these rules, and one draw needn't show every extreme that they name: `pattern`: in every block column, among the block rows held by one grid row (I congruent r modulo 8) at most 5 blocks are nonzero, exactly 5 in the grid row that holds the column's diagonal position; diagonal blocks of the window are always nonzero. `matrix`: diagonal blocks have diagonal entries between 21 and 51.
All inputs are finite; a program needn't handle non-finite values.
Results may differ from the reference program's by a relative error of at most 0.0008.
Values may be sent and summed in bfloat16 or wider, within the bound.
No kernel may reach another device: no remote copies, remote signals or barrier semaphores. Data moves between devices by JAX's collectives and lax.ppermute only.
A program may use at most 64 MiB of HBM per device.

```python
import jax
import jax.numpy as jnp
from jax import lax

BLK = 256
BR_DEV = 8
BC_DEV = 4
NEWTON = 3
NBR = 64
NBC = 128
MOST_NZ = 5
N_ROW = 8
N_COL = 32


def draw_matrix(key, part):
    total_rows = NBR * BLK
    total_cols = NBC * BLK
    key_noise = jax.random.fold_in(key, 11)
    key_pivot = jax.random.fold_in(key, 12)
    drawn = jnp.clip(jax.random.normal(key_noise, (total_rows, total_cols), jnp.float32), -6.0, 6.0)
    pivots = jax.random.uniform(key_pivot, (total_rows, 1), jnp.float32, 24.0, 48.0)
    row_pos = lax.broadcasted_iota(jnp.int32, (total_rows, total_cols), 0)
    col_pos = lax.broadcasted_iota(jnp.int32, (total_rows, total_cols), 1)
    on_block = row_pos // BLK == col_pos // BLK
    inside = 0.5 * drawn + jnp.where(row_pos == col_pos, pivots, 0.0)
    values = jnp.where(on_block, inside, drawn)
    grid_rows = NBR // BR_DEV
    grid_cols = NBC // BC_DEV
    return values.reshape(BR_DEV, grid_rows, BLK, BC_DEV, grid_cols, BLK).astype(jnp.bfloat16)


def draw_pattern(key, part):
    grid_rows = NBR // BR_DEV
    key_score = jax.random.fold_in(key, 21)
    key_count = jax.random.fold_in(key, 22)
    shape = (NBC, grid_rows, BR_DEV)
    local_pos = lax.broadcasted_iota(jnp.int32, shape, 2)
    grid_pos = lax.broadcasted_iota(jnp.int32, shape, 1)
    column_pos = lax.broadcasted_iota(jnp.int32, shape, 0)
    scores = jax.random.randint(key_score, shape, 0, 65536) * BR_DEV + local_pos
    block_row = local_pos * grid_rows + grid_pos
    scores = scores + jnp.where(block_row == column_pos, 1 << 24, 0)
    picked = jnp.argsort(-scores, axis=-1, stable=True)
    ranks = jnp.argsort(picked, axis=-1, stable=True)
    counts = jax.random.randint(key_count, (NBC, grid_rows), 1, MOST_NZ + 1)
    home = lax.broadcasted_iota(jnp.int32, (NBC, grid_rows), 0) % grid_rows
    which = lax.broadcasted_iota(jnp.int32, (NBC, grid_rows), 1)
    counts = jnp.where(which == home, MOST_NZ, counts)
    nonzero = (ranks < counts[:, :, None]).astype(jnp.int32)
    return jnp.transpose(nonzero, (2, 1, 0)).reshape(NBR, NBC)


def setup_inputs(seed: int = 0) -> dict:
    arg_keys = jax.random.split(jax.random.key(seed), 4)
    matrix = draw_matrix(jax.random.fold_in(arg_keys[3], 71), 0)
    pattern = draw_pattern(jax.random.fold_in(arg_keys[3], 71), 0)
    panel = jax.random.randint(arg_keys[2], (1,), 0, NBR - NBR // 4).astype(jnp.int32)
    return {"matrix": matrix, "pattern": pattern, "panel": panel}


def newton(pivot_block):
    identity = jnp.eye(BLK, dtype=jnp.float32)
    pivots = jnp.diagonal(pivot_block)
    inverse = identity / pivots[None, :]
    for sweep_index in range(NEWTON):
        image = jnp.dot(pivot_block, inverse, precision=lax.Precision.HIGHEST)
        inverse = jnp.dot(inverse, 2.0 * identity - image, precision=lax.Precision.HIGHEST)
    return inverse


def reference(matrix, pattern, panel):
    panel_at = panel[0]
    blocks = matrix.reshape(NBR, BLK, NBC, BLK)
    row_ids = jnp.arange(NBR, dtype=jnp.int32)
    col_ids = jnp.arange(NBC, dtype=jnp.int32)
    upper_row = lax.dynamic_index_in_dim(blocks, panel_at, 0, keepdims=False)
    mask_top = lax.dynamic_index_in_dim(pattern, panel_at, 0, keepdims=False)
    upper_keep = (mask_top * (col_ids > panel_at).astype(jnp.int32)).astype(jnp.bfloat16)
    upper_matrix = (upper_row * upper_keep[None, :, None]).reshape(BLK, NBC * BLK)
    pivot_block = lax.dynamic_index_in_dim(upper_row, panel_at, 1, keepdims=False).astype(jnp.float32)
    inverse = newton(pivot_block)
    panel_column = lax.dynamic_index_in_dim(blocks, panel_at, 2, keepdims=False)
    mask_left = lax.dynamic_index_in_dim(pattern, panel_at, 1, keepdims=False)
    lower_keep = (mask_left * (row_ids > panel_at).astype(jnp.int32)).astype(jnp.float32)
    scaled = (panel_column.astype(jnp.float32) * lower_keep[:, None, None]).reshape(NBR * BLK, BLK)
    lower_panel = jnp.dot(scaled, inverse, precision=lax.Precision.HIGHEST).reshape(NBR, BLK, BLK).astype(jnp.bfloat16)

    def update_row(packed):
        block_row, mask_row, lower_row, row_id = packed
        masked_base = block_row.astype(jnp.float32) * mask_row.astype(jnp.float32)[None, :, None]
        change = jnp.dot(lower_row, upper_matrix, preferred_element_type=jnp.float32).reshape(BLK, NBC, BLK)
        result = masked_base - change
        replaced = jnp.where(row_id > panel_at, lower_row.astype(jnp.float32), inverse)
        column_hit = (col_ids == panel_at) & (row_id >= panel_at)
        return jnp.where(column_hit[None, :, None], replaced[:, None, :], result)

    factored = lax.map(update_row, (blocks, pattern, lower_panel, row_ids))
    return factored.reshape(BR_DEV, N_ROW, BLK, BC_DEV, N_COL, BLK)
```

```python
import functools

import jax
import jax.numpy as jnp
from jax import lax
from jax.experimental import pallas as pl
from jax.experimental.pallas import tpu as pltpu
from jax.sharding import PartitionSpec as P

SLOTS = 5
BLK = 256
HI = lax.Precision.HIGHEST


def first(t):
    return t ^ 1


def second(t, n):
    return (t + 1) % n if t % 2 else (t - 1) % n


def second_of(t, n):
    return jnp.where(t % 2 == 1, t + 1, t + n - 1) % n


def spread_rows(block, scratch):
    for half in range(2):
        scratch[:, half * 4 : half * 4 + 4, :] = block[:, :, half * 128 : half * 128 + 128].astype(
            jnp.float32
        )


def pick_column(scratch, at, half):
    flat = scratch.reshape(BLK * 8, 128)
    return flat[pl.ds(half * 4 + at, BLK, stride=8), :].astype(jnp.bfloat16)


def top_kernel(info, block, upper, pivot, scratch):
    spread_rows(block[0], scratch)
    for half in range(2):
        lanes = slice(half * 128, half * 128 + 128)
        for at in range(4):
            upper[at, :, lanes] = pick_column(scratch, at, half)
        pivot[:, lanes] = pick_column(scratch, info[1], half)


def extract_top(matrix, info):
    return pl.pallas_call(
        top_kernel,
        grid_spec=pltpu.PrefetchScalarGridSpec(
            num_scalar_prefetch=1,
            grid=(1,),
            in_specs=[pl.BlockSpec((1, BLK, 4, BLK), lambda s, info: (info[0], 0, 0, 0))],
            out_specs=[
                pl.BlockSpec((4, BLK, BLK), lambda s, info: (0, 0, 0)),
                pl.BlockSpec((BLK, BLK), lambda s, info: (0, 0)),
            ],
            scratch_shapes=[pltpu.VMEM((BLK, 8, 128), jnp.float32)],
        ),
        out_shape=[
            jax.ShapeDtypeStruct((4, BLK, BLK), jnp.bfloat16),
            jax.ShapeDtypeStruct((BLK, BLK), jnp.bfloat16),
        ],
        name="extract_top",
    )(info, matrix)


def left_kernel(info, block, panel, scratch):
    spread_rows(block[0], scratch)
    for half in range(2):
        panel[0, :, half * 128 : half * 128 + 128] = pick_column(scratch, info[1], half)


def extract_left(matrix, info):
    return pl.pallas_call(
        left_kernel,
        grid_spec=pltpu.PrefetchScalarGridSpec(
            num_scalar_prefetch=1,
            grid=(SLOTS,),
            in_specs=[pl.BlockSpec((1, BLK, 4, BLK), lambda s, info: (info[2 + s], 0, 0, 0))],
            out_specs=pl.BlockSpec((1, BLK, BLK), lambda s, info: (s, 0, 0)),
            scratch_shapes=[pltpu.VMEM((BLK, 8, 128), jnp.float32)],
        ),
        out_shape=jax.ShapeDtypeStruct((SLOTS, BLK, BLK), jnp.bfloat16),
        name="extract_left",
    )(info, matrix)


def newton_kernel(pivot, panel, inverse, lower):
    block = pivot[...].astype(jnp.float32)
    down = lax.broadcasted_iota(jnp.int32, (BLK, BLK), 0)
    along = lax.broadcasted_iota(jnp.int32, (BLK, BLK), 1)
    same = down == along
    identity = jnp.where(same, 1.0, 0.0)
    diagonal = jnp.where(same, block, 0.0)
    error = identity - block * (1.0 / jnp.sum(diagonal, axis=0, keepdims=True))
    dot = functools.partial(jnp.dot, precision=HI, preferred_element_type=jnp.float32)
    error2 = dot(error, error)
    error4 = dot(error2, error2)
    left = identity + error
    left = left + dot(left, error2)
    left = left + dot(left, error4)
    result = left * (1.0 / jnp.sum(diagonal, axis=1, keepdims=True))
    inverse[...] = result
    high = result.astype(jnp.bfloat16)
    rest = result - high.astype(jnp.float32)
    middle = rest.astype(jnp.bfloat16)
    low = (rest - middle.astype(jnp.float32)).astype(jnp.bfloat16)
    for slot in range(SLOTS):
        rows = panel[slot]
        total = jnp.dot(rows, low, preferred_element_type=jnp.float32)
        total += jnp.dot(rows, middle, preferred_element_type=jnp.float32)
        total += jnp.dot(rows, high, preferred_element_type=jnp.float32)
        lower[slot] = total.astype(jnp.bfloat16)


def newton_lower(pivot, panel):
    return pl.pallas_call(
        newton_kernel,
        out_shape=[
            jax.ShapeDtypeStruct((BLK, BLK), jnp.float32),
            jax.ShapeDtypeStruct((SLOTS, BLK, BLK), jnp.bfloat16),
        ],
        name="newton_lower",
    )(pivot, panel)


def finish_kernel(mask, slot_of, keep, hit, block, lower, upper, inverse, out):
    row = pl.program_id(0)
    column = lax.broadcasted_iota(jnp.int32, (BLK, 4, 128), 1)
    on = jnp.zeros((BLK, 4, 128), jnp.int32)
    for at in range(4):
        on = jnp.where(column == at, mask[row * 4 + at], on)
    wide = out.reshape(BLK, 8, 128)
    for half in range(2):
        piece = block[0, :, :, half * 128 : half * 128 + 128].astype(jnp.float32)
        wide[:, pl.ds(half, 4, stride=2), :] = jnp.where(on != 0, piece, 0.0)
    slot = slot_of[row]

    for at in range(4):

        @pl.when((slot >= 0) & (keep[at] != 0))
        def _():
            change = jnp.dot(lower[slot], upper[at], preferred_element_type=jnp.float32)
            for half in range(2):
                rows = pl.ds(at * 2 + half, BLK, stride=8)
                out[rows, :] = out[rows, :] - change[:, half * 128 : half * 128 + 128]

        @pl.when((slot >= 0) & (hit[0] == at))
        def _():
            for half in range(2):
                out[pl.ds(at * 2 + half, BLK, stride=8), :] = lower[
                    slot, :, half * 128 : half * 128 + 128
                ].astype(jnp.float32)

        @pl.when((hit[1] == row) & (hit[0] == at))
        def _():
            for half in range(2):
                out[pl.ds(at * 2 + half, BLK, stride=8), :] = inverse[
                    :, half * 128 : half * 128 + 128
                ]


def finish(matrix, lower, upper, inverse, mask, slot_of, keep, hit):
    return pl.pallas_call(
        finish_kernel,
        grid_spec=pltpu.PrefetchScalarGridSpec(
            num_scalar_prefetch=4,
            grid=(8,),
            in_specs=[
                pl.BlockSpec((1, BLK, 4, BLK), lambda s, *_: (s, 0, 0, 0)),
                pl.BlockSpec((SLOTS, BLK, BLK), lambda s, *_: (0, 0, 0)),
                pl.BlockSpec((4, BLK, BLK), lambda s, *_: (0, 0, 0)),
                pl.BlockSpec((BLK, BLK), lambda s, *_: (0, 0)),
            ],
            out_specs=pl.BlockSpec((BLK * 8, 128), lambda s, *_: (s, 0)),
        ),
        out_shape=jax.ShapeDtypeStruct((8 * BLK * 8, 128), jnp.float32),
        name="finish",
        compiler_params=pltpu.CompilerParams(vmem_limit_bytes=32 * 1024 * 1024),
    )(mask, slot_of, keep, hit, matrix, lower, upper, inverse)


def places(size_row, size_col, core_zero, core_one):
    pairs = []
    for row in range(size_row):
        for at in range(size_col):
            to = (core_one if row % 2 else core_zero)(at // 8, at % 8)
            if to is not None:
                pairs.append((row * size_col + at, row * size_col + to[0] * 8 + to[1]))
    return pairs


def steps(parity):
    x1 = lambda x, z: (first(x), z)
    x2 = lambda x, z: (second(x, 4), z)
    mine = lambda z: z % 2 == parity
    z1 = lambda x, z: (x, first(z // 2) * 2 + parity) if mine(z) else None
    z2 = lambda x, z: (x, second(z // 2, 4) * 2 + parity) if mine(z) else None
    n1 = lambda x, z: (x, first(z))
    n2 = lambda x, z: (x, second(z, 8))
    across, along, last = (x1, x2), (z1, z2), (n1, n2)
    return [(across, along), (across, along), (along, across), (along, across), (last, last)]


def send_panel(parity, half_a, half_b, root_x, root_z):
    row, col = lax.axis_index("row"), lax.axis_index("col")
    sizes = lax.axis_size("row"), lax.axis_size("col")
    core, x, z = row % 2, col // 8, col % 8
    x_is = [x == root_x ^ 1, x == second_of(root_x, 4), x == root_x ^ 2]
    u, root_u = z // 2, root_z // 2
    z_is = [u == root_u ^ 1, u == second_of(root_u, 4), u == root_u ^ 2]
    early = [jnp.where(core == 0, a, b) for a, b in zip(x_is, z_is)]
    late = [jnp.where(core == 0, b, a) for a, b in zip(x_is, z_is)]
    plan = steps(parity)
    for step, (zero, one) in enumerate(plan):
        swap = step in (1, 3)
        got1 = lax.ppermute(half_b if swap else half_a, ("row", "col"), places(*sizes, zero[0], one[0]))
        got2 = lax.ppermute(half_a if swap else half_b, ("row", "col"), places(*sizes, zero[1], one[1]))
        near, far, opposite = early if step < 2 else late
        if step == 4:
            other = z % 2 != parity
            half_a, half_b = jnp.where(other, got1, half_a), jnp.where(other, got2, half_b)
        elif swap:
            half_b = jnp.where(near | opposite, got1, half_b)
            half_a = jnp.where(far | opposite, got2, half_a)
        else:
            half_a = jnp.where(near, got1, half_a)
            half_b = jnp.where(far, got2, half_b)
    return half_a, half_b


def row_pairs(size, to):
    return [(r, to(r // 2) * 2 + r % 2) for r in range(size)]


def body(matrix, pattern, panel):
    grid_row, grid_col = lax.axis_index("row"), lax.axis_index("col")
    rows_here, cols_here = lax.axis_size("row"), lax.axis_size("col")
    block_rows, order, block_cols = matrix.shape[0], matrix.shape[2], matrix.shape[3]
    at = panel[0]
    local = matrix.reshape(block_rows, order, block_cols, order)
    row_ids = jnp.arange(block_rows, dtype=jnp.int32) * rows_here + grid_row
    col_ids = jnp.arange(block_cols, dtype=jnp.int32) * cols_here + grid_col
    local_mask = lax.dynamic_index_in_dim(
        lax.dynamic_index_in_dim(
            pattern.reshape(block_rows, rows_here, block_cols, cols_here), grid_row, 1, keepdims=False
        ),
        grid_col,
        2,
        keepdims=False,
    )
    mask_top = lax.dynamic_index_in_dim(pattern, at, 0, keepdims=False).reshape(block_cols, cols_here)
    mask_top = lax.dynamic_index_in_dim(mask_top, grid_col, 1, keepdims=False)
    mask_left = lax.dynamic_index_in_dim(pattern, at, 1, keepdims=False).reshape(block_rows, rows_here)
    mask_left = lax.dynamic_index_in_dim(mask_left, grid_row, 1, keepdims=False)
    keep = ((mask_top != 0) & (col_ids > at)).astype(jnp.int32)
    used = (mask_left != 0) & (row_ids > at)
    count = jnp.cumsum(used.astype(jnp.int32))
    slot_of = jnp.where(used, count - 1, -1)
    numbers = jnp.arange(block_rows, dtype=jnp.int32)
    chosen = jnp.sum(
        jnp.where(slot_of[None, :] == jnp.arange(SLOTS, dtype=jnp.int32)[:, None], numbers[None, :], 0), axis=1
    )
    info = jnp.concatenate([jnp.stack([at // rows_here, at // cols_here]), chosen]).astype(jnp.int32)
    own_col = grid_col == at % cols_here
    hit = jnp.stack(
        [
            jnp.where(own_col, at // cols_here, -1),
            jnp.where(own_col & (grid_row == at % rows_here), at // rows_here, -1),
        ]
    ).astype(jnp.int32)
    col_hit = (jnp.arange(block_cols) == hit[0])[None, :] & (row_ids >= at)[:, None]
    mask = jnp.where(col_hit, 0, local_mask).reshape(-1).astype(jnp.int32)

    upper, pivot = extract_top(local, info)
    core, y = grid_row % 2, grid_row // 2
    root_core, root_y = at % rows_here % 2, at % rows_here // 2
    flip = [(r, r ^ 1) for r in range(rows_here)]
    y1 = row_pairs(rows_here, first)
    y2 = row_pairs(rows_here, lambda t: second(t, rows_here // 2))
    y3 = row_pairs(rows_here, lambda t: t ^ 2)
    y_is = [y == root_y ^ 1, y == second_of(root_y, 4), y == root_y ^ 2]

    pivot = jnp.where(core == root_core, pivot, lax.ppermute(pivot, "row", flip))
    pivot1, pivot2, pivot3 = (lax.ppermute(pivot, "row", p) for p in (y1, y2, y3))
    pivot = jnp.where(
        y_is[0], pivot1, jnp.where(y_is[1], pivot2, jnp.where(y_is[2], pivot3, pivot))
    )

    left = extract_left(local, info)
    inverse, lower = newton_lower(pivot, left)

    own = jnp.where(core == 0, upper[:2], upper[2:])
    other = jnp.where(core == 0, upper[2:], upper[:2])
    own = jnp.where(core == root_core, own, lax.ppermute(other, "row", flip))
    half_a, half_b = own[0], own[1]
    got1, got2 = lax.ppermute(half_a, "row", y1), lax.ppermute(half_b, "row", y2)
    half_a, half_b = jnp.where(y_is[0], got1, half_a), jnp.where(y_is[1], got2, half_b)
    got1, got2 = lax.ppermute(half_b, "row", y1), lax.ppermute(half_a, "row", y2)
    half_b = jnp.where(y_is[0] | y_is[2], got1, half_b)
    half_a = jnp.where(y_is[1] | y_is[2], got2, half_a)
    own = jnp.stack([half_a, half_b])
    other = lax.ppermute(own, "row", flip)
    upper = jnp.where(core == 0, jnp.concatenate([own, other]), jnp.concatenate([other, own]))

    flat = lower.reshape(2, SLOTS * order // 2, order)
    root_x, root_z = at % cols_here // 8, at % cols_here % 8
    half_a, half_b = lax.cond(
        root_z % 2 == 0,
        functools.partial(send_panel, 0),
        functools.partial(send_panel, 1),
        flat[0],
        flat[1],
        root_x,
        root_z,
    )
    lower = jnp.stack([half_a, half_b]).reshape(SLOTS, order, order)
    result = finish(local, lower, upper, inverse, mask, slot_of, keep, hit)
    return result.reshape(matrix.shape)


def solution(mesh):
    in_specs = (P(None, "row", None, None, "col", None), P(), P())
    out_specs = P(None, "row", None, None, "col", None)
    return jax.shard_map(body, mesh=mesh, in_specs=in_specs, out_specs=out_specs, check_vma=False)
```

```python
import functools

import jax
import jax.numpy as jnp
from jax import lax
from jax.experimental import pallas as pl
from jax.experimental.pallas import tpu as pltpu
from jax.sharding import PartitionSpec as P

SLOTS = 5
BLK = 256
HALF = 128
WIDE_Z = 8


def first(t):
    return t ^ 1


def second(t, n):
    return (t + 1) % n if t % 2 else (t - 1) % n


def second_of(t, n):
    return jnp.where(t % 2 == 1, t + 1, t + n - 1) % n


def lanes(half):
    return slice(half * HALF, half * HALF + HALF)


def spread_rows(block, scratch):
    for half in range(2):
        scratch[:, half * 4 : half * 4 + 4, :] = block[:, :, lanes(half)].astype(jnp.float32)


def pivot_kernel(panel, place, block, mine, other, scratch):
    spread_rows(block[0], scratch)
    flat = scratch.reshape(BLK * 8, HALF)
    at = lax.div(panel[0], place[2])
    for half in range(2):
        for out, core in ((mine, place[0]), (other, 1 - place[0])):
            start = core * (HALF * 8) + half * 4 + at
            out[:, lanes(half)] = flat[pl.ds(start, HALF, stride=8), :].astype(jnp.bfloat16)


def extract_pivot(matrix, panel, place):
    half = jax.ShapeDtypeStruct((HALF, BLK), jnp.bfloat16)
    return pl.pallas_call(
        pivot_kernel,
        grid_spec=pltpu.PrefetchScalarGridSpec(
            num_scalar_prefetch=2,
            grid=(1,),
            in_specs=[pl.BlockSpec((1, BLK, 4, BLK), lambda s, panel, place: (lax.div(panel[0], place[1]), 0, 0, 0))],
            out_specs=[pl.BlockSpec((HALF, BLK), lambda s, *_: (0, 0))] * 2,
            scratch_shapes=[pltpu.VMEM((BLK, 8, HALF), jnp.float32)],
        ),
        out_shape=[half, half],
        name="extract_pivot",
    )(panel, place, matrix)


def upper_kernel(panel, place, block, mine_a, mine_b, other_a, other_b, scratch):
    spread_rows(block[0], scratch)
    flat = scratch.reshape(BLK * 8, HALF)
    core = place[0]
    for out, at in ((other_a, 2 - 2 * core), (other_b, 3 - 2 * core), (mine_a, 2 * core), (mine_b, 2 * core + 1)):
        for half in range(2):
            out[:, lanes(half)] = flat[pl.ds(half * 4 + at, BLK, stride=8), :].astype(jnp.bfloat16)


def extract_upper(matrix, panel, place):
    block = jax.ShapeDtypeStruct((BLK, BLK), jnp.bfloat16)
    return pl.pallas_call(
        upper_kernel,
        grid_spec=pltpu.PrefetchScalarGridSpec(
            num_scalar_prefetch=2,
            grid=(1,),
            in_specs=[pl.BlockSpec((1, BLK, 4, BLK), lambda s, panel, place: (lax.div(panel[0], place[1]), 0, 0, 0))],
            out_specs=[pl.BlockSpec((BLK, BLK), lambda s, *_: (0, 0))] * 4,
            scratch_shapes=[pltpu.VMEM((BLK, 8, HALF), jnp.float32)],
        ),
        out_shape=[block] * 4,
        name="extract_upper",
    )(panel, place, matrix)


def mask_kernel(mask, slot_at, used, hit, block, out, panel):
    row = pl.program_id(0)
    column = lax.broadcasted_iota(jnp.int32, (BLK, 4, HALF), 1)
    on = jnp.zeros((BLK, 4, HALF), jnp.int32)
    for at in range(4):
        on = jnp.where(column == at, mask[row * 4 + at], on)
    wide = out.reshape(BLK, 8, HALF)
    for half in range(2):
        piece = block[0, :, :, lanes(half)].astype(jnp.float32)
        wide[:, pl.ds(half, 4, stride=2), :] = jnp.where(on != 0, piece, 0.0)

    @pl.when(used[row] != 0)
    def _():
        for half in range(2):
            panel[0, :, lanes(half)] = out[pl.ds(hit[2] * 2 + half, BLK, stride=8), :].astype(jnp.bfloat16)

    @pl.when((hit[0] >= 0) & (row >= hit[3]))
    def _():
        for half in range(2):
            out[pl.ds(hit[2] * 2 + half, BLK, stride=8), :] = jnp.zeros((BLK, HALF), jnp.float32)


def mask_all(matrix, mask, slot_at, used, hit):
    return pl.pallas_call(
        mask_kernel,
        grid_spec=pltpu.PrefetchScalarGridSpec(
            num_scalar_prefetch=4,
            grid=(8,),
            in_specs=[pl.BlockSpec((1, BLK, 4, BLK), lambda s, *_: (s, 0, 0, 0))],
            out_specs=[
                pl.BlockSpec((BLK * 8, HALF), lambda s, *_: (s, 0)),
                pl.BlockSpec((1, BLK, BLK), lambda s, mask, slot_at, used, hit: (slot_at[s], 0, 0)),
            ],
        ),
        out_shape=[
            jax.ShapeDtypeStruct((8 * BLK * 8, HALF), jnp.float32),
            jax.ShapeDtypeStruct((SLOTS, BLK, BLK), jnp.bfloat16),
        ],
        name="mask_all",
        compiler_params=pltpu.CompilerParams(vmem_limit_bytes=24 * 1024 * 1024),
    )(mask, slot_at, used, hit, matrix)


def halves(value):
    high = value.astype(jnp.bfloat16)
    return high, (value - high.astype(jnp.float32)).astype(jnp.bfloat16)


def product(left, right):
    (left_high, left_low), (right_high, right_low) = left, right
    dot = functools.partial(jnp.dot, preferred_element_type=jnp.float32)
    return dot(left_high, right_high) + (dot(left_high, right_low) + dot(left_low, right_high))


def newton_kernel(place, mine, other, panel, inverse, lower_a, lower_b):
    own, rest = mine[...].astype(jnp.float32), other[...].astype(jnp.float32)
    zero = place[0] == 0
    block = jnp.concatenate([jnp.where(zero, own, rest), jnp.where(zero, rest, own)], axis=0)
    down = lax.broadcasted_iota(jnp.int32, (BLK, BLK), 0)
    along = lax.broadcasted_iota(jnp.int32, (BLK, BLK), 1)
    same = down == along
    identity = jnp.where(same, 1.0, 0.0)
    diagonal = jnp.where(same, block, 0.0)
    error = identity - block * (1.0 / jnp.sum(diagonal, axis=0, keepdims=True))
    error_parts = halves(error)
    error2 = product(error_parts, error_parts)
    error2_parts = halves(error2)
    error4 = product(error2_parts, error2_parts)
    left = identity + error
    left = left + error2 + product(error_parts, error2_parts)
    left = left + product(halves(left), halves(error4))
    result = left * (1.0 / jnp.sum(diagonal, axis=1, keepdims=True))
    inverse[...] = result
    high, low = halves(result)
    for slot in range(SLOTS):
        rows = panel[slot]
        total = jnp.dot(rows, low, preferred_element_type=jnp.float32)
        total += jnp.dot(rows, high, preferred_element_type=jnp.float32)
        lower_a[slot] = total[:HALF].astype(jnp.bfloat16)
        lower_b[slot] = total[HALF:].astype(jnp.bfloat16)


def newton_lower(place, mine, other, panel):
    half = jax.ShapeDtypeStruct((SLOTS, HALF, BLK), jnp.bfloat16)
    return pl.pallas_call(
        newton_kernel,
        in_specs=[pl.BlockSpec(memory_space=pltpu.SMEM)] + [pl.BlockSpec(memory_space=pltpu.VMEM)] * 3,
        out_shape=[jax.ShapeDtypeStruct((BLK, BLK), jnp.float32), half, half],
        name="newton_lower",
    )(place, mine, other, panel)


def update_kernel(rows, keep, hit, place, base, lower_a, lower_b, mine_a, mine_b, other_a, other_b, inverse, out):
    step = pl.program_id(0)
    row = rows[step]
    before = rows[jnp.maximum(step - 1, 0)]

    @pl.when((step == 0) | (row != before))
    def _():
        out[...] = base[...]

    live = (step > 0) & (step <= hit[4])
    slot = jnp.maximum(step - 1, 0)
    core = place[0]
    for at in range(4):
        own, others = ((mine_a, other_a), (mine_b, other_b))[at % 2]

        @pl.when(live & (keep[at] != 0))
        def _():
            right = jnp.where(core == at // 2, own[...], others[...])
            for part, lower in enumerate((lower_a, lower_b)):
                change = jnp.dot(lower[slot], right, preferred_element_type=jnp.float32)
                for half in range(2):
                    into = pl.ds(part * HALF * 8 + at * 2 + half, HALF, stride=8)
                    out[into, :] = out[into, :] - change[:, lanes(half)]

    @pl.when(live & (hit[0] >= 0))
    def _():
        for part, lower in enumerate((lower_a, lower_b)):
            for half in range(2):
                into = pl.ds(part * HALF * 8 + hit[2] * 2 + half, HALF, stride=8)
                out[into, :] = lower[slot, :, lanes(half)].astype(jnp.float32)

    @pl.when((step == 0) & (hit[1] != 0))
    def _():
        for half in range(2):
            out[pl.ds(hit[2] * 2 + half, BLK, stride=8), :] = inverse[:, lanes(half)]


def update(base, rows, keep, hit, place, lower, upper, inverse):
    whole = lambda *shape: pl.BlockSpec(shape, lambda s, *_: (0,) * len(shape))
    return pl.pallas_call(
        update_kernel,
        grid_spec=pltpu.PrefetchScalarGridSpec(
            num_scalar_prefetch=4,
            grid=(SLOTS + 1,),
            in_specs=[pl.BlockSpec((BLK * 8, HALF), lambda s, rows, *_: (rows[s], 0))]
            + [whole(SLOTS, HALF, BLK)] * 2
            + [whole(BLK, BLK)] * 5,
            out_specs=pl.BlockSpec((BLK * 8, HALF), lambda s, rows, *_: (rows[s], 0)),
        ),
        out_shape=jax.ShapeDtypeStruct(base.shape, jnp.float32),
        input_output_aliases={4: 0},
        name="update",
        compiler_params=pltpu.CompilerParams(vmem_limit_bytes=24 * 1024 * 1024),
    )(rows, keep, hit, place, base, *lower, *upper, inverse)


def places(size_row, size_col, core_zero, core_one):
    pairs = []
    for row in range(size_row):
        for at in range(size_col):
            to = (core_one if row % 2 else core_zero)(at // 8, at % 8)
            if to is not None:
                pairs.append((row * size_col + at, row * size_col + to[0] * 8 + to[1]))
    return pairs


def steps(parity):
    x1 = lambda x, z: (first(x), z)
    x2 = lambda x, z: (second(x, 4), z)
    mine = lambda z: z % 2 == parity
    z1 = lambda x, z: (x, first(z // 2) * 2 + parity) if mine(z) else None
    z2 = lambda x, z: (x, second(z // 2, 4) * 2 + parity) if mine(z) else None
    n1 = lambda x, z: (x, first(z))
    n2 = lambda x, z: (x, second(z, 8))
    across, along, last = (x1, x2), (z1, z2), (n1, n2)
    return [(across, along), (across, along), (along, across), (along, across), (last, last)]


def send_panel(parity, half_a, half_b, root_x, root_z):
    row, col = lax.axis_index("row"), lax.axis_index("col")
    sizes = lax.axis_size("row"), lax.axis_size("col")
    core, x, z = row % 2, col // 8, col % 8
    x_is = [x == root_x ^ 1, x == second_of(root_x, 4), x == root_x ^ 2]
    u, root_u = z // 2, root_z // 2
    z_is = [u == root_u ^ 1, u == second_of(root_u, 4), u == root_u ^ 2]
    early = [jnp.where(core == 0, a, b) for a, b in zip(x_is, z_is)]
    late = [jnp.where(core == 0, b, a) for a, b in zip(x_is, z_is)]
    plan = steps(parity)
    for step, (zero, one) in enumerate(plan):
        swap = step in (1, 3)
        got1 = lax.ppermute(half_b if swap else half_a, ("row", "col"), places(*sizes, zero[0], one[0]))
        got2 = lax.ppermute(half_a if swap else half_b, ("row", "col"), places(*sizes, zero[1], one[1]))
        near, far, opposite = early if step < 2 else late
        if step == 4:
            other = z % 2 != parity
            half_a, half_b = jnp.where(other, got1, half_a), jnp.where(other, got2, half_b)
        elif swap:
            half_b = jnp.where(near | opposite, got1, half_b)
            half_a = jnp.where(far | opposite, got2, half_a)
        else:
            half_a = jnp.where(near, got1, half_a)
            half_b = jnp.where(far, got2, half_b)
    return half_a, half_b


def body(matrix, pattern, panel):
    grid_row, grid_col = lax.axis_index("row"), lax.axis_index("col")
    rows_here, cols_here = lax.axis_size("row"), lax.axis_size("col")
    block_rows, order, block_cols = matrix.shape[0], matrix.shape[2], matrix.shape[3]
    at = panel[0]
    local = matrix.reshape(block_rows, order, block_cols, order)
    core, y = grid_row % 2, grid_row // 2
    root_core, root_y = at % rows_here % 2, at % rows_here // 2
    tall = rows_here // 2
    at_y = (y - root_y + tall) % tall
    place = jnp.stack([core, jnp.int32(rows_here), jnp.int32(cols_here)]).astype(jnp.int32)
    flip = [(r, r ^ 1) for r in range(rows_here)]
    shift = lambda value, by: lax.ppermute(
        value, "row", [(r, (r + 2 * by) % rows_here) for r in range(rows_here)]
    )
    cross = lambda value: lax.ppermute(value, "row", flip)

    pivot, pivot_other = extract_pivot(local, panel, place)
    pivot = jnp.where(core == root_core, pivot, cross(pivot_other))
    up, down, over = shift(pivot, 1), shift(pivot, -1), shift(pivot, 2)
    pivot = jnp.where(at_y == 1, up, jnp.where(at_y == 3, down, jnp.where(at_y == 2, over, pivot)))
    pivot_other = cross(pivot)

    row_ids = jnp.arange(block_rows, dtype=jnp.int32) * rows_here + grid_row
    col_ids = jnp.arange(block_cols, dtype=jnp.int32) * cols_here + grid_col
    local_mask = lax.dynamic_index_in_dim(
        lax.dynamic_index_in_dim(
            pattern.reshape(block_rows, rows_here, block_cols, cols_here), grid_row, 1, keepdims=False
        ),
        grid_col,
        2,
        keepdims=False,
    )
    mask = local_mask.reshape(-1).astype(jnp.int32)
    mask_top = lax.dynamic_index_in_dim(pattern, at, 0, keepdims=False).reshape(block_cols, cols_here)
    mask_top = lax.dynamic_index_in_dim(mask_top, grid_col, 1, keepdims=False)
    mask_left = lax.dynamic_index_in_dim(pattern, at, 1, keepdims=False).reshape(block_rows, rows_here)
    mask_left = lax.dynamic_index_in_dim(mask_left, grid_row, 1, keepdims=False)
    keep = ((mask_top != 0) & (col_ids > at)).astype(jnp.int32)
    used = ((mask_left != 0) & (row_ids > at)).astype(jnp.int32)
    numbers = jnp.arange(block_rows, dtype=jnp.int32)
    reached = jnp.sum(jnp.where(numbers[None, :] <= numbers[:, None], used[None, :], 0), axis=1)
    count = jnp.sum(used)
    slot_at = jnp.maximum(reached - 1, 0).astype(jnp.int32)
    owner_col = grid_col == at % cols_here
    owner = owner_col & (grid_row == at % rows_here)
    wanted = jnp.minimum(jnp.arange(SLOTS + 1, dtype=jnp.int32), count)
    wanted = jnp.where(wanted == 0, jnp.minimum(count, 1), wanted)
    rows = jnp.sum(
        jnp.where((reached[None, :] == wanted[:, None]) & (used[None, :] != 0), numbers[None, :], 0), axis=1
    )
    pivot_row = at // rows_here
    rows = jnp.where((jnp.arange(SLOTS + 1) == 0) | (count == 0), jnp.where(owner, pivot_row, rows), rows)
    rows = rows.astype(jnp.int32)
    first_below = (at - grid_row + rows_here - 1) // rows_here
    hit = jnp.stack(
        [jnp.where(owner_col, 1, -1), jnp.where(owner, 1, 0), at // cols_here, first_below, count]
    ).astype(jnp.int32)

    upper_a, upper_b, other_a, other_b = extract_upper(local, panel, place)
    from_a, from_b = cross(other_a), cross(other_b)
    upper_a = jnp.where(core == root_core, upper_a, from_a)
    upper_b = jnp.where(core == root_core, upper_b, from_b)
    up, down = shift(upper_a, 1), shift(upper_b, -1)
    upper_a, upper_b = jnp.where(at_y == 1, up, upper_a), jnp.where(at_y == 3, down, upper_b)
    is_root = at_y == 0
    up = shift(jnp.where(is_root, upper_b, upper_a), 1)
    down = shift(jnp.where(is_root, upper_a, upper_b), -1)
    upper_a = jnp.where(at_y == 2, up, jnp.where(at_y == 3, down, upper_a))
    upper_b = jnp.where(at_y == 1, up, jnp.where(at_y == 2, down, upper_b))
    other_a, other_b = cross(upper_a), cross(upper_b)

    base, left = mask_all(local, mask, slot_at, used, hit)
    inverse, lower_a, lower_b = newton_lower(place, pivot, pivot_other, left)

    root = at % cols_here
    root_x, root_z = root // WIDE_Z, root % WIDE_Z
    lower = lax.cond(
        root_z % 2 == 0,
        functools.partial(send_panel, 0),
        functools.partial(send_panel, 1),
        lower_a,
        lower_b,
        root_x,
        root_z,
    )
    result = update(base, rows, keep, hit, place, lower, (upper_a, upper_b, other_a, other_b), inverse)
    return result.reshape(matrix.shape)


def solution(mesh):
    in_specs = (P(None, "row", None, None, "col", None), P(), P())
    out_specs = P(None, "row", None, None, "col", None)
    return jax.shard_map(body, mesh=mesh, in_specs=in_specs, out_specs=out_specs, check_vma=False)
```

```python
import functools

import jax
import jax.numpy as jnp
from jax import lax
from jax.experimental import pallas as pl
from jax.experimental.pallas import tpu as pltpu
from jax.sharding import PartitionSpec as P

SLOTS = 5
BLK = 256
HALF = 128
WIDE_Z = 8


def first(t):
    return t ^ 1


def second(t, n):
    return (t + 1) % n if t % 2 else (t - 1) % n


def second_of(t, n):
    return jnp.where(t % 2 == 1, t + 1, t + n - 1) % n


def lanes(half):
    return slice(half * HALF, half * HALF + HALF)


def spread_rows(block, scratch):
    for half in range(2):
        scratch[:, half * 4 : half * 4 + 4, :] = block[:, :, lanes(half)].astype(jnp.float32)


def pivot_kernel(panel, place, block, mine, other, scratch):
    spread_rows(block[0], scratch)
    flat = scratch.reshape(BLK * 8, HALF)
    at = lax.div(panel[0], place[2])
    for half in range(2):
        for out, core in ((mine, place[0]), (other, 1 - place[0])):
            start = core * (HALF * 8) + half * 4 + at
            out[:, lanes(half)] = flat[pl.ds(start, HALF, stride=8), :].astype(jnp.bfloat16)


def extract_pivot(matrix, panel, place):
    half = jax.ShapeDtypeStruct((HALF, BLK), jnp.bfloat16)
    return pl.pallas_call(
        pivot_kernel,
        grid_spec=pltpu.PrefetchScalarGridSpec(
            num_scalar_prefetch=2,
            grid=(1,),
            in_specs=[pl.BlockSpec((1, BLK, 4, BLK), lambda s, panel, place: (lax.div(panel[0], place[1]), 0, 0, 0))],
            out_specs=[pl.BlockSpec((HALF, BLK), lambda s, *_: (0, 0))] * 2,
            scratch_shapes=[pltpu.VMEM((BLK, 8, HALF), jnp.float32)],
        ),
        out_shape=[half, half],
        name="extract_pivot",
    )(panel, place, matrix)


def upper_kernel(panel, place, block, after, mine_a, mine_b, other_a, other_b, scratch):
    spread_rows(block[0], scratch)
    flat = scratch.reshape(BLK * 8, HALF)
    core = place[0]
    for out, at in ((other_a, 2 - 2 * core), (other_b, 3 - 2 * core), (mine_a, 2 * core), (mine_b, 2 * core + 1)):
        for half in range(2):
            out[:, lanes(half)] = flat[pl.ds(half * 4 + at, BLK, stride=8), :].astype(jnp.bfloat16)


def extract_upper(matrix, panel, place, after):
    block = jax.ShapeDtypeStruct((BLK, BLK), jnp.bfloat16)
    return pl.pallas_call(
        upper_kernel,
        grid_spec=pltpu.PrefetchScalarGridSpec(
            num_scalar_prefetch=2,
            grid=(1,),
            in_specs=[pl.BlockSpec((1, BLK, 4, BLK), lambda s, panel, place: (lax.div(panel[0], place[1]), 0, 0, 0)), pl.BlockSpec(memory_space=pl.ANY)],
            out_specs=[pl.BlockSpec((BLK, BLK), lambda s, *_: (0, 0))] * 4,
            scratch_shapes=[pltpu.VMEM((BLK, 8, HALF), jnp.float32)],
        ),
        out_shape=[block] * 4,
        name="extract_upper",
    )(panel, place, matrix, after)


def mask_kernel(mask, slot_at, used, hit, block, out, panel):
    row = pl.program_id(0)
    column = lax.broadcasted_iota(jnp.int32, (BLK, 4, HALF), 1)
    on = jnp.zeros((BLK, 4, HALF), jnp.int32)
    for at in range(4):
        on = jnp.where(column == at, mask[row * 4 + at], on)
    wide = out.reshape(BLK, 8, HALF)
    for half in range(2):
        piece = block[0, :, :, lanes(half)].astype(jnp.float32)
        wide[:, pl.ds(half, 4, stride=2), :] = jnp.where(on != 0, piece, 0.0)

    @pl.when(used[row] != 0)
    def _():
        for half in range(2):
            panel[0, :, lanes(half)] = out[pl.ds(hit[2] * 2 + half, BLK, stride=8), :].astype(jnp.bfloat16)

    @pl.when((hit[0] >= 0) & (row >= hit[3]))
    def _():
        for half in range(2):
            out[pl.ds(hit[2] * 2 + half, BLK, stride=8), :] = jnp.zeros((BLK, HALF), jnp.float32)


def mask_all(matrix, mask, slot_at, used, hit):
    return pl.pallas_call(
        mask_kernel,
        grid_spec=pltpu.PrefetchScalarGridSpec(
            num_scalar_prefetch=4,
            grid=(8,),
            in_specs=[pl.BlockSpec((1, BLK, 4, BLK), lambda s, *_: (s, 0, 0, 0))],
            out_specs=[
                pl.BlockSpec((BLK * 8, HALF), lambda s, *_: (s, 0)),
                pl.BlockSpec((1, BLK, BLK), lambda s, mask, slot_at, used, hit: (slot_at[s], 0, 0)),
            ],
        ),
        out_shape=[
            jax.ShapeDtypeStruct((8 * BLK * 8, HALF), jnp.float32),
            jax.ShapeDtypeStruct((SLOTS, BLK, BLK), jnp.bfloat16),
        ],
        name="mask_all",
        cost_estimate=pl.CostEstimate(flops=4 << 20, bytes_accessed=20 << 20, transcendentals=0),
        compiler_params=pltpu.CompilerParams(vmem_limit_bytes=24 * 1024 * 1024),
    )(mask, slot_at, used, hit, matrix)


def halves(value):
    high = value.astype(jnp.bfloat16)
    return high, (value - high.astype(jnp.float32)).astype(jnp.bfloat16)


def product(left, right):
    (left_high, left_low), (right_high, right_low) = left, right
    dot = functools.partial(jnp.dot, preferred_element_type=jnp.float32)
    return dot(left_high, right_high) + (dot(left_high, right_low) + dot(left_low, right_high))


def newton_kernel(place, mine, other, panel, inverse, lower_a, lower_b):
    own, rest = mine[...].astype(jnp.float32), other[...].astype(jnp.float32)
    zero = place[0] == 0
    block = jnp.concatenate([jnp.where(zero, own, rest), jnp.where(zero, rest, own)], axis=0)
    down = lax.broadcasted_iota(jnp.int32, (BLK, BLK), 0)
    along = lax.broadcasted_iota(jnp.int32, (BLK, BLK), 1)
    same = down == along
    identity = jnp.where(same, 1.0, 0.0)
    diagonal = jnp.where(same, block, 0.0)
    error = identity - block * (1.0 / jnp.sum(diagonal, axis=0, keepdims=True))
    error_parts = halves(error)
    error2 = product(error_parts, error_parts)
    error2_parts = halves(error2)
    error4 = product(error2_parts, error2_parts)
    left = identity + error
    left = left + error2 + product(error_parts, error2_parts)
    left = left + product(halves(left), halves(error4))
    result = left * (1.0 / jnp.sum(diagonal, axis=1, keepdims=True))
    inverse[...] = result
    high, low = halves(result)
    for slot in range(SLOTS):
        rows = panel[slot]
        total = jnp.dot(rows, low, preferred_element_type=jnp.float32)
        total += jnp.dot(rows, high, preferred_element_type=jnp.float32)
        lower_a[slot] = total[:HALF].astype(jnp.bfloat16)
        lower_b[slot] = total[HALF:].astype(jnp.bfloat16)


def newton_lower(place, mine, other, panel):
    half = jax.ShapeDtypeStruct((SLOTS, HALF, BLK), jnp.bfloat16)
    return pl.pallas_call(
        newton_kernel,
        in_specs=[pl.BlockSpec(memory_space=pltpu.SMEM)] + [pl.BlockSpec(memory_space=pltpu.VMEM)] * 3,
        out_shape=[jax.ShapeDtypeStruct((BLK, BLK), jnp.float32), half, half],
        name="newton_lower",
    )(place, mine, other, panel)


def update_kernel(rows, keep, hit, place, base, lower_a, lower_b, mine_a, mine_b, other_a, other_b, inverse, out):
    step = pl.program_id(0)
    row = rows[step]
    before = rows[jnp.maximum(step - 1, 0)]

    @pl.when((step == 0) | (row != before))
    def _():
        out[...] = base[...]

    live = (step > 0) & (step <= hit[4])
    slot = jnp.maximum(step - 1, 0)
    core = place[0]
    for at in range(4):
        own, others = ((mine_a, other_a), (mine_b, other_b))[at % 2]

        @pl.when(live & (keep[at] != 0))
        def _():
            right = jnp.where(core == at // 2, own[...], others[...])
            for part, lower in enumerate((lower_a, lower_b)):
                change = jnp.dot(lower[slot], right, preferred_element_type=jnp.float32)
                for half in range(2):
                    into = pl.ds(part * HALF * 8 + at * 2 + half, HALF, stride=8)
                    out[into, :] = out[into, :] - change[:, lanes(half)]

    @pl.when(live & (hit[0] >= 0))
    def _():
        for part, lower in enumerate((lower_a, lower_b)):
            for half in range(2):
                into = pl.ds(part * HALF * 8 + hit[2] * 2 + half, HALF, stride=8)
                out[into, :] = lower[slot, :, lanes(half)].astype(jnp.float32)

    @pl.when((step == 0) & (hit[1] != 0))
    def _():
        for half in range(2):
            out[pl.ds(hit[2] * 2 + half, BLK, stride=8), :] = inverse[:, lanes(half)]


def update(base, rows, keep, hit, place, lower, upper, inverse):
    whole = lambda *shape: pl.BlockSpec(shape, lambda s, *_: (0,) * len(shape))
    return pl.pallas_call(
        update_kernel,
        grid_spec=pltpu.PrefetchScalarGridSpec(
            num_scalar_prefetch=4,
            grid=(SLOTS + 1,),
            in_specs=[pl.BlockSpec((BLK * 8, HALF), lambda s, rows, *_: (rows[s], 0))]
            + [whole(SLOTS, HALF, BLK)] * 2
            + [whole(BLK, BLK)] * 5,
            out_specs=pl.BlockSpec((BLK * 8, HALF), lambda s, rows, *_: (rows[s], 0)),
        ),
        out_shape=jax.ShapeDtypeStruct(base.shape, jnp.float32),
        input_output_aliases={4: 0},
        name="update",
        compiler_params=pltpu.CompilerParams(vmem_limit_bytes=24 * 1024 * 1024),
    )(rows, keep, hit, place, base, *lower, *upper, inverse)


def places(size_row, size_col, core_zero, core_one):
    pairs = []
    for row in range(size_row):
        for at in range(size_col):
            to = (core_one if row % 2 else core_zero)(at // 8, at % 8)
            if to is not None:
                pairs.append((row * size_col + at, row * size_col + to[0] * 8 + to[1]))
    return pairs


def steps(parity):
    x1 = lambda x, z: (first(x), z)
    x2 = lambda x, z: (second(x, 4), z)
    mine = lambda z: z % 2 == parity
    z1 = lambda x, z: (x, first(z // 2) * 2 + parity) if mine(z) else None
    z2 = lambda x, z: (x, second(z // 2, 4) * 2 + parity) if mine(z) else None
    n1 = lambda x, z: (x, first(z))
    n2 = lambda x, z: (x, second(z, 8))
    across, along, last = (x1, x2), (z1, z2), (n1, n2)
    return [(across, along), (across, along), (along, across), (along, across), (last, last)]


def row_moves(rows):
    flip = [(r, r ^ 1) for r in range(rows)]
    shift = lambda value, by: lax.ppermute(value, "row", [(r, (r + 2 * by) % rows) for r in range(rows)])
    return lambda value: lax.ppermute(value, "row", flip), shift


def send_all(parity, half_a, half_b, upper_a, upper_b, root_x, root_z, at_y):
    row, col = lax.axis_index("row"), lax.axis_index("col")
    sizes = lax.axis_size("row"), lax.axis_size("col")
    cross, shift = row_moves(sizes[0])
    core, x, z = row % 2, col // WIDE_Z, col % WIDE_Z
    x_is = [x == root_x ^ 1, x == second_of(root_x, 4), x == root_x ^ 2]
    u, root_u = z // 2, root_z // 2
    z_is = [u == root_u ^ 1, u == second_of(root_u, 4), u == root_u ^ 2]
    early = [jnp.where(core == 0, a, b) for a, b in zip(x_is, z_is)]
    late = [jnp.where(core == 0, b, a) for a, b in zip(x_is, z_is)]
    is_root = at_y == 0
    for step, (zero, one) in enumerate(steps(parity)):
        swap = step in (1, 3)
        got1 = lax.ppermute(half_b if swap else half_a, ("row", "col"), places(*sizes, zero[0], one[0]))
        got2 = lax.ppermute(half_a if swap else half_b, ("row", "col"), places(*sizes, zero[1], one[1]))
        near, far, opposite = early if step < 2 else late
        if step == 0:
            upper_a, got1 = lax.optimization_barrier((upper_a, got1))
            up, down = shift(upper_a, 1), shift(upper_b, -1)
            upper_a, upper_b = jnp.where(at_y == 1, up, upper_a), jnp.where(at_y == 3, down, upper_b)
        if step == 1:
            upper_a, got1 = lax.optimization_barrier((upper_a, got1))
            up = shift(jnp.where(is_root, upper_b, upper_a), 1)
            down = shift(jnp.where(is_root, upper_a, upper_b), -1)
            upper_a = jnp.where(at_y == 2, up, jnp.where(at_y == 3, down, upper_a))
            upper_b = jnp.where(at_y == 1, up, jnp.where(at_y == 2, down, upper_b))
        if step == 3:
            upper_a, got1 = lax.optimization_barrier((upper_a, got1))
            other_a, other_b = cross(upper_a), cross(upper_b)
        if step == 4:
            other = z % 2 != parity
            half_a, half_b = jnp.where(other, got1, half_a), jnp.where(other, got2, half_b)
        elif swap:
            half_b = jnp.where(near | opposite, got1, half_b)
            half_a = jnp.where(far | opposite, got2, half_a)
        else:
            half_a = jnp.where(near, got1, half_a)
            half_b = jnp.where(far, got2, half_b)
    return half_a, half_b, upper_a, upper_b, other_a, other_b


def body(matrix, pattern, panel):
    grid_row, grid_col = lax.axis_index("row"), lax.axis_index("col")
    rows_here, cols_here = lax.axis_size("row"), lax.axis_size("col")
    block_rows, order, block_cols = matrix.shape[0], matrix.shape[2], matrix.shape[3]
    at = panel[0]
    local = matrix.reshape(block_rows, order, block_cols, order)
    core, y = grid_row % 2, grid_row // 2
    root_core, root_y = at % rows_here % 2, at % rows_here // 2
    tall = rows_here // 2
    at_y = (y - root_y + tall) % tall
    place = jnp.stack([core, jnp.int32(rows_here), jnp.int32(cols_here)]).astype(jnp.int32)
    cross, shift = row_moves(rows_here)

    pivot, pivot_other = extract_pivot(local, panel, place)
    pivot = jnp.where(core == root_core, pivot, cross(pivot_other))

    row_ids = jnp.arange(block_rows, dtype=jnp.int32) * rows_here + grid_row
    col_ids = jnp.arange(block_cols, dtype=jnp.int32) * cols_here + grid_col
    local_mask = lax.dynamic_index_in_dim(
        lax.dynamic_index_in_dim(
            pattern.reshape(block_rows, rows_here, block_cols, cols_here), grid_row, 1, keepdims=False
        ),
        grid_col,
        2,
        keepdims=False,
    )
    mask = local_mask.reshape(-1).astype(jnp.int32)
    mask_top = lax.dynamic_index_in_dim(pattern, at, 0, keepdims=False).reshape(block_cols, cols_here)
    mask_top = lax.dynamic_index_in_dim(mask_top, grid_col, 1, keepdims=False)
    mask_left = lax.dynamic_index_in_dim(pattern, at, 1, keepdims=False).reshape(block_rows, rows_here)
    mask_left = lax.dynamic_index_in_dim(mask_left, grid_row, 1, keepdims=False)
    keep = ((mask_top != 0) & (col_ids > at)).astype(jnp.int32)
    used = ((mask_left != 0) & (row_ids > at)).astype(jnp.int32)
    numbers = jnp.arange(block_rows, dtype=jnp.int32)
    reached = jnp.sum(jnp.where(numbers[None, :] <= numbers[:, None], used[None, :], 0), axis=1)
    count = jnp.sum(used)
    slot_at = jnp.maximum(reached - 1, 0).astype(jnp.int32)
    owner_col = grid_col == at % cols_here
    owner = owner_col & (grid_row == at % rows_here)
    wanted = jnp.minimum(jnp.arange(SLOTS + 1, dtype=jnp.int32), count)
    wanted = jnp.where(wanted == 0, jnp.minimum(count, 1), wanted)
    rows = jnp.sum(
        jnp.where((reached[None, :] == wanted[:, None]) & (used[None, :] != 0), numbers[None, :], 0), axis=1
    )
    pivot_row = at // rows_here
    rows = jnp.where((jnp.arange(SLOTS + 1) == 0) | (count == 0), jnp.where(owner, pivot_row, rows), rows)
    rows = rows.astype(jnp.int32)
    first_below = (at - grid_row + rows_here - 1) // rows_here
    hit = jnp.stack(
        [jnp.where(owner_col, 1, -1), jnp.where(owner, 1, 0), at // cols_here, first_below, count]
    ).astype(jnp.int32)

    up, down, over = shift(pivot, 1), shift(pivot, -1), shift(pivot, 2)
    upper_a, upper_b, other_a, other_b = extract_upper(local, panel, place, pivot)
    base, left = mask_all(local, mask, slot_at, used, hit)
    pivot = jnp.where(at_y == 1, up, jnp.where(at_y == 3, down, jnp.where(at_y == 2, over, pivot)))
    pivot_other = cross(pivot)
    from_a, from_b = cross(other_a), cross(other_b)
    inverse, lower_a, lower_b = newton_lower(place, pivot, pivot_other, left)
    upper_a = jnp.where(core == root_core, upper_a, from_a)
    upper_b = jnp.where(core == root_core, upper_b, from_b)

    root = at % cols_here
    root_x, root_z = root // WIDE_Z, root % WIDE_Z
    *lower, upper_a, upper_b, other_a, other_b = lax.cond(
        root_z % 2 == 0,
        functools.partial(send_all, 0),
        functools.partial(send_all, 1),
        lower_a,
        lower_b,
        upper_a,
        upper_b,
        root_x,
        root_z,
        at_y,
    )
    result = update(base, rows, keep, hit, place, lower, (upper_a, upper_b, other_a, other_b), inverse)
    return result.reshape(matrix.shape)


def solution(mesh):
    in_specs = (P(None, "row", None, None, "col", None), P(), P())
    out_specs = P(None, "row", None, None, "col", None)
    return jax.shard_map(body, mesh=mesh, in_specs=in_specs, out_specs=out_specs, check_vma=False)
```

```python
import functools

import jax
import jax.numpy as jnp
from jax import lax
from jax.experimental import pallas as pl
from jax.experimental.pallas import tpu as pltpu
from jax.sharding import PartitionSpec as P

SLOTS = 5
BLK = 256
HALF = 128
WIDE_Z = 8
MASK, SLOT, USED, ROWS, KEEP, HIT, CORE, WAY = 0, 32, 40, 48, 54, 58, 63, 64


def first(t):
    return t ^ 1


def second(t, n):
    return (t + 1) % n if t % 2 else (t - 1) % n


def second_of(t, n):
    return jnp.where(t % 2 == 1, t + 1, t + n - 1) % n


def lanes(half):
    return slice(half * HALF, half * HALF + HALF)


def spread_rows(block, scratch):
    for half in range(2):
        scratch[:, half * 4 : half * 4 + 4, :] = block[:, :, lanes(half)].astype(jnp.float32)


def pivot_kernel(panel, place, block, mine, other, scratch):
    spread_rows(block[0], scratch)
    flat = scratch.reshape(BLK * 8, HALF)
    at = lax.div(panel[0], place[2])
    for half in range(2):
        for out, core in ((mine, place[0]), (other, 1 - place[0])):
            start = core * (HALF * 8) + half * 4 + at
            out[:, lanes(half)] = flat[pl.ds(start, HALF, stride=8), :].astype(jnp.bfloat16)


def extract_pivot(matrix, panel, place):
    half = jax.ShapeDtypeStruct((HALF, BLK), jnp.bfloat16)
    return pl.pallas_call(
        pivot_kernel,
        grid_spec=pltpu.PrefetchScalarGridSpec(
            num_scalar_prefetch=2,
            grid=(1,),
            in_specs=[pl.BlockSpec((1, BLK, 4, BLK), lambda s, panel, place: (lax.div(panel[0], place[1]), 0, 0, 0))],
            out_specs=[pl.BlockSpec((HALF, BLK), lambda s, *_: (0, 0))] * 2,
            scratch_shapes=[pltpu.VMEM((BLK, 8, HALF), jnp.float32)],
        ),
        out_shape=[half, half],
        name="extract_pivot",
    )(panel, place, matrix)


def upper_kernel(panel, place, block, after, mine_a, mine_b, other_a, other_b, scratch):
    spread_rows(block[0], scratch)
    flat = scratch.reshape(BLK * 8, HALF)
    core = place[0]
    for out, at in ((other_a, 2 - 2 * core), (other_b, 3 - 2 * core), (mine_a, 2 * core), (mine_b, 2 * core + 1)):
        for half in range(2):
            out[:, lanes(half)] = flat[pl.ds(half * 4 + at, BLK, stride=8), :].astype(jnp.bfloat16)


def extract_upper(matrix, panel, place, after):
    block = jax.ShapeDtypeStruct((BLK, BLK), jnp.bfloat16)
    return pl.pallas_call(
        upper_kernel,
        grid_spec=pltpu.PrefetchScalarGridSpec(
            num_scalar_prefetch=2,
            grid=(1,),
            in_specs=[pl.BlockSpec((1, BLK, 4, BLK), lambda s, panel, place: (lax.div(panel[0], place[1]), 0, 0, 0)), pl.BlockSpec(memory_space=pl.ANY)],
            out_specs=[pl.BlockSpec((BLK, BLK), lambda s, *_: (0, 0))] * 4,
            scratch_shapes=[pltpu.VMEM((BLK, 8, HALF), jnp.float32)],
        ),
        out_shape=[block] * 4,
        name="extract_upper",
    )(panel, place, matrix, after)


def plan_kernel(panel, pattern, place, after, info):
    at, rows, cols, grid_row, grid_col = panel[0], place[1], place[2], place[3], place[4]
    in_col = lax.rem(at, cols) == grid_col
    owner = in_col & (lax.rem(at, rows) == grid_row)
    used, reached, count = [], [], jnp.int32(0)
    for i in range(8):
        row = i * rows + grid_row
        here = ((pattern[row, at] != 0) & (row > at)).astype(jnp.int32)
        count = count + here
        used.append(here)
        reached.append(count)
        info[USED + i] = here
        info[SLOT + i] = jnp.maximum(count - 1, 0)
        for j in range(4):
            info[MASK + i * 4 + j] = pattern[row, j * cols + grid_col]
    for step in range(SLOTS + 1):
        wanted = jnp.minimum(max(step, 1), count)
        found = jnp.int32(0)
        for i in range(8):
            found = jnp.where((used[i] != 0) & (reached[i] == wanted), i, found)
        own = owner if step == 0 else owner & (count == 0)
        info[ROWS + step] = jnp.where(own, lax.div(at, rows), found)
    for j in range(4):
        column = j * cols + grid_col
        info[KEEP + j] = ((pattern[at, column] != 0) & (column > at)).astype(jnp.int32)
    info[HIT] = jnp.where(in_col, 1, -1)
    info[HIT + 1] = owner.astype(jnp.int32)
    info[HIT + 2] = lax.div(at, cols)
    info[HIT + 3] = lax.div(at - grid_row + rows - 1, rows)
    info[HIT + 4] = count
    info[CORE] = place[0]
    info[WAY] = place[5]


def plan_blocks(panel, pattern, place, after):
    scalars = pl.BlockSpec(memory_space=pltpu.SMEM)
    return pl.pallas_call(
        plan_kernel,
        in_specs=[scalars] * 3 + [pl.BlockSpec(memory_space=pl.ANY)],
        out_specs=scalars,
        out_shape=jax.ShapeDtypeStruct((72,), jnp.int32),
        name="plan_blocks",
    )(panel, pattern, place, after)


def mask_kernel(info, block, out, panel, way):
    row = pl.program_id(0)
    way[0] = info[WAY]
    column = lax.broadcasted_iota(jnp.int32, (BLK, 4, HALF), 1)
    on = jnp.zeros((BLK, 4, HALF), jnp.int32)
    for at in range(4):
        on = jnp.where(column == at, info[MASK + row * 4 + at], on)
    wide = out.reshape(BLK, 8, HALF)
    for half in range(2):
        piece = block[0, :, :, lanes(half)].astype(jnp.float32)
        wide[:, pl.ds(half, 4, stride=2), :] = jnp.where(on != 0, piece, 0.0)

    @pl.when(info[USED + row] != 0)
    def _():
        for half in range(2):
            panel[0, :, lanes(half)] = out[pl.ds(info[HIT + 2] * 2 + half, BLK, stride=8), :].astype(jnp.bfloat16)

    @pl.when((info[HIT] >= 0) & (row >= info[HIT + 3]))
    def _():
        for half in range(2):
            out[pl.ds(info[HIT + 2] * 2 + half, BLK, stride=8), :] = jnp.zeros((BLK, HALF), jnp.float32)


def mask_all(matrix, info):
    return pl.pallas_call(
        mask_kernel,
        grid_spec=pltpu.PrefetchScalarGridSpec(
            num_scalar_prefetch=1,
            grid=(8,),
            in_specs=[pl.BlockSpec((1, BLK, 4, BLK), lambda s, *_: (s, 0, 0, 0))],
            out_specs=[
                pl.BlockSpec((BLK * 8, HALF), lambda s, *_: (s, 0)),
                pl.BlockSpec((1, BLK, BLK), lambda s, info: (info[SLOT + s], 0, 0)),
                pl.BlockSpec(memory_space=pltpu.SMEM),
            ],
        ),
        out_shape=[
            jax.ShapeDtypeStruct((8 * BLK * 8, HALF), jnp.float32),
            jax.ShapeDtypeStruct((SLOTS, BLK, BLK), jnp.bfloat16),
            jax.ShapeDtypeStruct((1,), jnp.int32),
        ],
        name="mask_all",
        cost_estimate=pl.CostEstimate(flops=4 << 20, bytes_accessed=20 << 20, transcendentals=0),
        compiler_params=pltpu.CompilerParams(vmem_limit_bytes=24 * 1024 * 1024),
    )(info, matrix)


def halves(value):
    high = value.astype(jnp.bfloat16)
    return high, (value - high.astype(jnp.float32)).astype(jnp.bfloat16)


def product(left, right):
    (left_high, left_low), (right_high, right_low) = left, right
    dot = functools.partial(jnp.dot, preferred_element_type=jnp.float32)
    return dot(left_high, right_high) + (dot(left_high, right_low) + dot(left_low, right_high))


def newton_kernel(place, mine, other, panel, inverse, lower_a, lower_b):
    own, rest = mine[...].astype(jnp.float32), other[...].astype(jnp.float32)
    zero = place[0] == 0
    block = jnp.concatenate([jnp.where(zero, own, rest), jnp.where(zero, rest, own)], axis=0)
    down = lax.broadcasted_iota(jnp.int32, (BLK, BLK), 0)
    along = lax.broadcasted_iota(jnp.int32, (BLK, BLK), 1)
    same = down == along
    identity = jnp.where(same, 1.0, 0.0)
    diagonal = jnp.where(same, block, 0.0)
    error = identity - block * (1.0 / jnp.sum(diagonal, axis=0, keepdims=True))
    error_parts = halves(error)
    error2 = product(error_parts, error_parts)
    error2_parts = halves(error2)
    error4 = product(error2_parts, error2_parts)
    left = identity + error
    left = left + error2 + product(error_parts, error2_parts)
    left = left + product(halves(left), halves(error4))
    result = left * (1.0 / jnp.sum(diagonal, axis=1, keepdims=True))
    inverse[...] = result
    high, low = halves(result)
    for slot in range(SLOTS):
        rows = panel[slot]
        total = jnp.dot(rows, low, preferred_element_type=jnp.float32)
        total += jnp.dot(rows, high, preferred_element_type=jnp.float32)
        lower_a[slot] = total[:HALF].astype(jnp.bfloat16)
        lower_b[slot] = total[HALF:].astype(jnp.bfloat16)


def newton_lower(place, mine, other, panel):
    half = jax.ShapeDtypeStruct((SLOTS, HALF, BLK), jnp.bfloat16)
    return pl.pallas_call(
        newton_kernel,
        in_specs=[pl.BlockSpec(memory_space=pltpu.SMEM)] + [pl.BlockSpec(memory_space=pltpu.VMEM)] * 3,
        out_shape=[jax.ShapeDtypeStruct((BLK, BLK), jnp.float32), half, half],
        name="newton_lower",
    )(place, mine, other, panel)


def update_kernel(info, base, lower_a, lower_b, mine_a, mine_b, other_a, other_b, inverse, out):
    step = pl.program_id(0)
    row = info[ROWS + step]
    before = info[ROWS + jnp.maximum(step - 1, 0)]

    @pl.when((step == 0) | (row != before))
    def _():
        out[...] = base[...]

    live = (step > 0) & (step <= info[HIT + 4])
    slot = jnp.maximum(step - 1, 0)
    core = info[CORE]
    for at in range(4):
        own, others = ((mine_a, other_a), (mine_b, other_b))[at % 2]

        @pl.when(live & (info[KEEP + at] != 0))
        def _():
            right = jnp.where(core == at // 2, own[...], others[...])
            for part, lower in enumerate((lower_a, lower_b)):
                change = jnp.dot(lower[slot], right, preferred_element_type=jnp.float32)
                for half in range(2):
                    into = pl.ds(part * HALF * 8 + at * 2 + half, HALF, stride=8)
                    out[into, :] = out[into, :] - change[:, lanes(half)]

    @pl.when(live & (info[HIT] >= 0))
    def _():
        for part, lower in enumerate((lower_a, lower_b)):
            for half in range(2):
                into = pl.ds(part * HALF * 8 + info[HIT + 2] * 2 + half, HALF, stride=8)
                out[into, :] = lower[slot, :, lanes(half)].astype(jnp.float32)

    @pl.when((step == 0) & (info[HIT + 1] != 0))
    def _():
        for half in range(2):
            out[pl.ds(info[HIT + 2] * 2 + half, BLK, stride=8), :] = inverse[:, lanes(half)]


def update(base, info, lower, upper, inverse):
    whole = lambda *shape: pl.BlockSpec(shape, lambda s, *_: (0,) * len(shape))
    return pl.pallas_call(
        update_kernel,
        grid_spec=pltpu.PrefetchScalarGridSpec(
            num_scalar_prefetch=1,
            grid=(SLOTS + 1,),
            in_specs=[pl.BlockSpec((BLK * 8, HALF), lambda s, info: (info[ROWS + s], 0))]
            + [whole(SLOTS, HALF, BLK)] * 2
            + [whole(BLK, BLK)] * 5,
            out_specs=pl.BlockSpec((BLK * 8, HALF), lambda s, info: (info[ROWS + s], 0)),
        ),
        out_shape=jax.ShapeDtypeStruct(base.shape, jnp.float32),
        input_output_aliases={1: 0},
        name="update",
        compiler_params=pltpu.CompilerParams(vmem_limit_bytes=24 * 1024 * 1024),
    )(info, base, *lower, *upper, inverse)


def places(size_row, size_col, core_zero, core_one):
    pairs = []
    for row in range(size_row):
        for at in range(size_col):
            to = (core_one if row % 2 else core_zero)(at // 8, at % 8)
            if to is not None:
                pairs.append((row * size_col + at, row * size_col + to[0] * 8 + to[1]))
    return pairs


def steps(parity):
    x1 = lambda x, z: (first(x), z)
    x2 = lambda x, z: (second(x, 4), z)
    mine = lambda z: z % 2 == parity
    z1 = lambda x, z: (x, first(z // 2) * 2 + parity) if mine(z) else None
    z2 = lambda x, z: (x, second(z // 2, 4) * 2 + parity) if mine(z) else None
    n1 = lambda x, z: (x, first(z))
    n2 = lambda x, z: (x, second(z, 8))
    across, along, last = (x1, x2), (z1, z2), (n1, n2)
    return [(across, along), (across, along), (along, across), (along, across), (last, last)]


def row_moves(rows):
    flip = [(r, r ^ 1) for r in range(rows)]
    shift = lambda value, by: lax.ppermute(value, "row", [(r, (r + 2 * by) % rows) for r in range(rows)])
    return lambda value: lax.ppermute(value, "row", flip), shift


def send_all(parity, local, panel, place, half_a, half_b, root_x, root_z, root_core, at_y):
    row, col = lax.axis_index("row"), lax.axis_index("col")
    sizes = lax.axis_size("row"), lax.axis_size("col")
    cross, shift = row_moves(sizes[0])
    core, x, z = row % 2, col // WIDE_Z, col % WIDE_Z
    x_is = [x == root_x ^ 1, x == second_of(root_x, 4), x == root_x ^ 2]
    u, root_u = z // 2, root_z // 2
    z_is = [u == root_u ^ 1, u == second_of(root_u, 4), u == root_u ^ 2]
    early = [jnp.where(core == 0, a, b) for a, b in zip(x_is, z_is)]
    late = [jnp.where(core == 0, b, a) for a, b in zip(x_is, z_is)]
    is_root = at_y == 0
    for step, (zero, one) in enumerate(steps(parity)):
        swap = step in (1, 3)
        got1 = lax.ppermute(half_b if swap else half_a, ("row", "col"), places(*sizes, zero[0], one[0]))
        got2 = lax.ppermute(half_a if swap else half_b, ("row", "col"), places(*sizes, zero[1], one[1]))
        near, far, opposite = early if step < 2 else late
        if step == 0:
            upper_a, upper_b, other_a, other_b = extract_upper(local, panel, place, got1[0, :16, :HALF])
            from_a, from_b = cross(other_a), cross(other_b)
            upper_a = jnp.where(core == root_core, upper_a, from_a)
            upper_b = jnp.where(core == root_core, upper_b, from_b)
            up, down = shift(upper_a, 1), shift(upper_b, -1)
            upper_a, upper_b = jnp.where(at_y == 1, up, upper_a), jnp.where(at_y == 3, down, upper_b)
        if step == 1:
            upper_a, got1 = lax.optimization_barrier((upper_a, got1))
            up = shift(jnp.where(is_root, upper_b, upper_a), 1)
            down = shift(jnp.where(is_root, upper_a, upper_b), -1)
            upper_a = jnp.where(at_y == 2, up, jnp.where(at_y == 3, down, upper_a))
            upper_b = jnp.where(at_y == 1, up, jnp.where(at_y == 2, down, upper_b))
        if step == 3:
            upper_a, got1 = lax.optimization_barrier((upper_a, got1))
            other_a, other_b = cross(upper_a), cross(upper_b)
        if step == 4:
            other = z % 2 != parity
            half_a, half_b = jnp.where(other, got1, half_a), jnp.where(other, got2, half_b)
        elif swap:
            half_b = jnp.where(near | opposite, got1, half_b)
            half_a = jnp.where(far | opposite, got2, half_a)
        else:
            half_a = jnp.where(near, got1, half_a)
            half_b = jnp.where(far, got2, half_b)
    return half_a, half_b, upper_a, upper_b, other_a, other_b


def body(matrix, pattern, panel):
    grid_row, grid_col = lax.axis_index("row"), lax.axis_index("col")
    rows_here, cols_here = lax.axis_size("row"), lax.axis_size("col")
    block_rows, order, block_cols = matrix.shape[0], matrix.shape[2], matrix.shape[3]
    at = panel[0]
    local = matrix.reshape(block_rows, order, block_cols, order)
    core, y = grid_row % 2, grid_row // 2
    root_core, root_y = at % rows_here % 2, at % rows_here // 2
    tall = rows_here // 2
    at_y = (y - root_y + tall) % tall
    place = jnp.stack([core, jnp.int32(rows_here), jnp.int32(cols_here), grid_row, grid_col, at_y]).astype(jnp.int32)
    cross, shift = row_moves(rows_here)

    pivot, pivot_other = extract_pivot(local, panel, place)
    pivot = jnp.where(core == root_core, pivot, cross(pivot_other))

    info = plan_blocks(panel, pattern, place, pivot)
    up, down, over = shift(pivot, 1), shift(pivot, -1), shift(pivot, 2)
    base, left, way = mask_all(local, info)
    way = way[0]
    pivot = jnp.where(way == 1, up, jnp.where(way == 3, down, jnp.where(way == 2, over, pivot)))
    pivot_other = cross(pivot)
    inverse, lower_a, lower_b = newton_lower(place, pivot, pivot_other, left)

    root = at % cols_here
    root_x, root_z = root // WIDE_Z, root % WIDE_Z
    *lower, upper_a, upper_b, other_a, other_b = lax.cond(
        root_z % 2 == 0,
        functools.partial(send_all, 0),
        functools.partial(send_all, 1),
        local,
        panel,
        place,
        lower_a,
        lower_b,
        root_x,
        root_z,
        root_core,
        at_y,
    )
    result = update(base, info, lower, (upper_a, upper_b, other_a, other_b), inverse)
    return result.reshape(matrix.shape)


def solution(mesh):
    in_specs = (P(None, "row", None, None, "col", None), P(), P())
    out_specs = P(None, "row", None, None, "col", None)
    return jax.shard_map(body, mesh=mesh, in_specs=in_specs, out_specs=out_specs, check_vma=False)
```

```python
import functools

import jax
import jax.numpy as jnp
from jax import lax
from jax.experimental import pallas as pl
from jax.experimental.pallas import tpu as pltpu
from jax.sharding import PartitionSpec as P

SLOTS = 5
BLK = 256
HALF = 128
WIDE_Z = 8
MASK, SLOT, USED, ROWS, KEEP, HIT, CORE = 0, 32, 40, 48, 54, 58, 63


def first(t):
    return t ^ 1


def second(t, n):
    return (t + 1) % n if t % 2 else (t - 1) % n


def second_of(t, n):
    return jnp.where(t % 2 == 1, t + 1, t + n - 1) % n


def lanes(half):
    return slice(half * HALF, half * HALF + HALF)


def spread_rows(block, scratch):
    for half in range(2):
        scratch[:, half * 4 : half * 4 + 4, :] = block[:, :, lanes(half)].astype(jnp.float32)


def pivot_kernel(panel, place, block, mine, other, scratch):
    spread_rows(block[0], scratch)
    flat = scratch.reshape(BLK * 8, HALF)
    at = lax.div(panel[0], place[2])
    for half in range(2):
        for out, core in ((mine, place[0]), (other, 1 - place[0])):
            start = core * (HALF * 8) + half * 4 + at
            out[:, lanes(half)] = flat[pl.ds(start, HALF, stride=8), :].astype(jnp.bfloat16)


def extract_pivot(matrix, panel, place):
    half = jax.ShapeDtypeStruct((HALF, BLK), jnp.bfloat16)
    return pl.pallas_call(
        pivot_kernel,
        grid_spec=pltpu.PrefetchScalarGridSpec(
            num_scalar_prefetch=2,
            grid=(1,),
            in_specs=[pl.BlockSpec((1, BLK, 4, BLK), lambda s, panel, place: (lax.div(panel[0], place[1]), 0, 0, 0))],
            out_specs=[pl.BlockSpec((HALF, BLK), lambda s, *_: (0, 0))] * 2,
            scratch_shapes=[pltpu.VMEM((BLK, 8, HALF), jnp.float32)],
        ),
        out_shape=[half, half],
        name="extract_pivot",
    )(panel, place, matrix)


def upper_kernel(panel, place, block, after, mine_a, mine_b, other_a, other_b, way, scratch):
    way[0] = place[5]
    spread_rows(block[0], scratch)
    flat = scratch.reshape(BLK * 8, HALF)
    core = place[0]
    for out, at in ((other_a, 2 - 2 * core), (other_b, 3 - 2 * core), (mine_a, 2 * core), (mine_b, 2 * core + 1)):
        for half in range(2):
            out[:, lanes(half)] = flat[pl.ds(half * 4 + at, BLK, stride=8), :].astype(jnp.bfloat16)


def extract_upper(matrix, panel, place, after):
    block = jax.ShapeDtypeStruct((BLK, BLK), jnp.bfloat16)
    return pl.pallas_call(
        upper_kernel,
        grid_spec=pltpu.PrefetchScalarGridSpec(
            num_scalar_prefetch=2,
            grid=(1,),
            in_specs=[pl.BlockSpec((1, BLK, 4, BLK), lambda s, panel, place: (lax.div(panel[0], place[1]), 0, 0, 0)), pl.BlockSpec(memory_space=pl.ANY)],
            out_specs=[pl.BlockSpec((BLK, BLK), lambda s, *_: (0, 0))] * 4 + [pl.BlockSpec(memory_space=pltpu.SMEM)],
            scratch_shapes=[pltpu.VMEM((BLK, 8, HALF), jnp.float32)],
        ),
        out_shape=[block] * 4 + [jax.ShapeDtypeStruct((1,), jnp.int32)],
        name="extract_upper",
    )(panel, place, matrix, after)


def plan_kernel(panel, pattern, place, after, info):
    at, rows, cols, grid_row, grid_col = panel[0], place[1], place[2], place[3], place[4]
    in_col = lax.rem(at, cols) == grid_col
    owner = in_col & (lax.rem(at, rows) == grid_row)
    used, reached, count = [], [], jnp.int32(0)
    for i in range(8):
        row = i * rows + grid_row
        here = ((pattern[row, at] != 0) & (row > at)).astype(jnp.int32)
        count = count + here
        used.append(here)
        reached.append(count)
        info[USED + i] = here
        info[SLOT + i] = jnp.maximum(count - 1, 0)
        for j in range(4):
            info[MASK + i * 4 + j] = pattern[row, j * cols + grid_col]
    for step in range(SLOTS + 1):
        wanted = jnp.minimum(max(step, 1), count)
        found = jnp.int32(0)
        for i in range(8):
            found = jnp.where((used[i] != 0) & (reached[i] == wanted), i, found)
        own = owner if step == 0 else owner & (count == 0)
        info[ROWS + step] = jnp.where(own, lax.div(at, rows), found)
    for j in range(4):
        column = j * cols + grid_col
        info[KEEP + j] = ((pattern[at, column] != 0) & (column > at)).astype(jnp.int32)
    info[HIT] = jnp.where(in_col, 1, -1)
    info[HIT + 1] = owner.astype(jnp.int32)
    info[HIT + 2] = lax.div(at, cols)
    info[HIT + 3] = lax.div(at - grid_row + rows - 1, rows)
    info[HIT + 4] = count
    info[CORE] = place[0]


def plan_blocks(panel, pattern, place, after):
    scalars = pl.BlockSpec(memory_space=pltpu.SMEM)
    return pl.pallas_call(
        plan_kernel,
        in_specs=[scalars] * 3 + [pl.BlockSpec(memory_space=pl.ANY)],
        out_specs=scalars,
        out_shape=jax.ShapeDtypeStruct((64,), jnp.int32),
        name="plan_blocks",
    )(panel, pattern, place, after)


def mask_kernel(info, block, out, panel):
    row = pl.program_id(0)
    column = lax.broadcasted_iota(jnp.int32, (BLK, 4, HALF), 1)
    on = jnp.zeros((BLK, 4, HALF), jnp.int32)
    for at in range(4):
        on = jnp.where(column == at, info[MASK + row * 4 + at], on)
    wide = out.reshape(BLK, 8, HALF)
    for half in range(2):
        piece = block[0, :, :, lanes(half)].astype(jnp.float32)
        wide[:, pl.ds(half, 4, stride=2), :] = jnp.where(on != 0, piece, 0.0)

    @pl.when(info[USED + row] != 0)
    def _():
        for half in range(2):
            panel[0, :, lanes(half)] = out[pl.ds(info[HIT + 2] * 2 + half, BLK, stride=8), :].astype(jnp.bfloat16)

    @pl.when((info[HIT] >= 0) & (row >= info[HIT + 3]))
    def _():
        for half in range(2):
            out[pl.ds(info[HIT + 2] * 2 + half, BLK, stride=8), :] = jnp.zeros((BLK, HALF), jnp.float32)


def mask_all(matrix, info):
    return pl.pallas_call(
        mask_kernel,
        grid_spec=pltpu.PrefetchScalarGridSpec(
            num_scalar_prefetch=1,
            grid=(8,),
            in_specs=[pl.BlockSpec((1, BLK, 4, BLK), lambda s, *_: (s, 0, 0, 0))],
            out_specs=[
                pl.BlockSpec((BLK * 8, HALF), lambda s, *_: (s, 0)),
                pl.BlockSpec((1, BLK, BLK), lambda s, info: (info[SLOT + s], 0, 0)),
            ],
        ),
        out_shape=[
            jax.ShapeDtypeStruct((8 * BLK * 8, HALF), jnp.float32),
            jax.ShapeDtypeStruct((SLOTS, BLK, BLK), jnp.bfloat16),
        ],
        name="mask_all",
        cost_estimate=pl.CostEstimate(flops=4 << 20, bytes_accessed=20 << 20, transcendentals=0),
        compiler_params=pltpu.CompilerParams(vmem_limit_bytes=24 * 1024 * 1024),
    )(info, matrix)


def halves(value):
    high = value.astype(jnp.bfloat16)
    return high, (value - high.astype(jnp.float32)).astype(jnp.bfloat16)


def product(left, right):
    (left_high, left_low), (right_high, right_low) = left, right
    dot = functools.partial(jnp.dot, preferred_element_type=jnp.float32)
    return dot(left_high, right_high) + (dot(left_high, right_low) + dot(left_low, right_high))


def newton_kernel(place, mine, other, panel, inverse, lower_a, lower_b):
    own, rest = mine[...].astype(jnp.float32), other[...].astype(jnp.float32)
    zero = place[0] == 0
    block = jnp.concatenate([jnp.where(zero, own, rest), jnp.where(zero, rest, own)], axis=0)
    down = lax.broadcasted_iota(jnp.int32, (BLK, BLK), 0)
    along = lax.broadcasted_iota(jnp.int32, (BLK, BLK), 1)
    same = down == along
    identity = jnp.where(same, 1.0, 0.0)
    diagonal = jnp.where(same, block, 0.0)
    error = identity - block * (1.0 / jnp.sum(diagonal, axis=0, keepdims=True))
    error_parts = halves(error)
    error2 = product(error_parts, error_parts)
    error2_parts = halves(error2)
    error4 = product(error2_parts, error2_parts)
    left = identity + error
    left = left + error2 + product(error_parts, error2_parts)
    left = left + product(halves(left), halves(error4))
    result = left * (1.0 / jnp.sum(diagonal, axis=1, keepdims=True))
    inverse[...] = result
    high, low = halves(result)
    for slot in range(SLOTS):
        rows = panel[slot]
        total = jnp.dot(rows, low, preferred_element_type=jnp.float32)
        total += jnp.dot(rows, high, preferred_element_type=jnp.float32)
        lower_a[slot] = total[:HALF].astype(jnp.bfloat16)
        lower_b[slot] = total[HALF:].astype(jnp.bfloat16)


def newton_lower(place, mine, other, panel):
    half = jax.ShapeDtypeStruct((SLOTS, HALF, BLK), jnp.bfloat16)
    return pl.pallas_call(
        newton_kernel,
        in_specs=[pl.BlockSpec(memory_space=pltpu.SMEM)] + [pl.BlockSpec(memory_space=pltpu.VMEM)] * 3,
        out_shape=[jax.ShapeDtypeStruct((BLK, BLK), jnp.float32), half, half],
        name="newton_lower",
    )(place, mine, other, panel)


def update_kernel(info, base, lower_a, lower_b, mine_a, mine_b, other_a, other_b, inverse, out):
    step = pl.program_id(0)
    row = info[ROWS + step]
    before = info[ROWS + jnp.maximum(step - 1, 0)]

    @pl.when((step == 0) | (row != before))
    def _():
        out[...] = base[...]

    live = (step > 0) & (step <= info[HIT + 4])
    slot = jnp.maximum(step - 1, 0)
    core = info[CORE]
    for at in range(4):
        own, others = ((mine_a, other_a), (mine_b, other_b))[at % 2]

        @pl.when(live & (info[KEEP + at] != 0))
        def _():
            right = jnp.where(core == at // 2, own[...], others[...])
            left = jnp.concatenate([lower_a[slot], lower_b[slot]], axis=0)
            change = jnp.dot(left, right, preferred_element_type=jnp.float32)
            for half in range(2):
                into = pl.ds(at * 2 + half, BLK, stride=8)
                out[into, :] = base[into, :] - change[:, lanes(half)]

    @pl.when(live & (info[HIT] >= 0))
    def _():
        for part, lower in enumerate((lower_a, lower_b)):
            for half in range(2):
                into = pl.ds(part * HALF * 8 + info[HIT + 2] * 2 + half, HALF, stride=8)
                out[into, :] = lower[slot, :, lanes(half)].astype(jnp.float32)

    @pl.when((step == 0) & (info[HIT + 1] != 0))
    def _():
        for half in range(2):
            out[pl.ds(info[HIT + 2] * 2 + half, BLK, stride=8), :] = inverse[:, lanes(half)]


def update(base, info, lower, upper, inverse):
    whole = lambda *shape: pl.BlockSpec(shape, lambda s, *_: (0,) * len(shape))
    return pl.pallas_call(
        update_kernel,
        grid_spec=pltpu.PrefetchScalarGridSpec(
            num_scalar_prefetch=1,
            grid=(SLOTS + 1,),
            in_specs=[pl.BlockSpec((BLK * 8, HALF), lambda s, info: (info[ROWS + s], 0))]
            + [whole(SLOTS, HALF, BLK)] * 2
            + [whole(BLK, BLK)] * 5,
            out_specs=pl.BlockSpec((BLK * 8, HALF), lambda s, info: (info[ROWS + s], 0)),
        ),
        out_shape=jax.ShapeDtypeStruct(base.shape, jnp.float32),
        input_output_aliases={1: 0},
        name="update",
        compiler_params=pltpu.CompilerParams(vmem_limit_bytes=24 * 1024 * 1024),
    )(info, base, *lower, *upper, inverse)


def places(size_row, size_col, core_zero, core_one):
    pairs = []
    for row in range(size_row):
        for at in range(size_col):
            to = (core_one if row % 2 else core_zero)(at // 8, at % 8)
            if to is not None:
                pairs.append((row * size_col + at, row * size_col + to[0] * 8 + to[1]))
    return pairs


def steps(parity):
    x1 = lambda x, z: (first(x), z)
    x2 = lambda x, z: (second(x, 4), z)
    mine = lambda z: z % 2 == parity
    z1 = lambda x, z: (x, first(z // 2) * 2 + parity) if mine(z) else None
    z2 = lambda x, z: (x, second(z // 2, 4) * 2 + parity) if mine(z) else None
    n1 = lambda x, z: (x, first(z))
    n2 = lambda x, z: (x, second(z, 8))
    across, along, last = (x1, x2), (z1, z2), (n1, n2)
    return [(across, along), (across, along), (along, across), (along, across), (last, last)]


def row_moves(rows):
    flip = [(r, r ^ 1) for r in range(rows)]
    shift = lambda value, by: lax.ppermute(value, "row", [(r, (r + 2 * by) % rows) for r in range(rows)])
    return lambda value: lax.ppermute(value, "row", flip), shift


def send_all(parity, half_a, half_b, upper_a, upper_b, root_x, root_z, at_y):
    row, col = lax.axis_index("row"), lax.axis_index("col")
    sizes = lax.axis_size("row"), lax.axis_size("col")
    cross, shift = row_moves(sizes[0])
    core, x, z = row % 2, col // WIDE_Z, col % WIDE_Z
    x_is = [x == root_x ^ 1, x == second_of(root_x, 4), x == root_x ^ 2]
    u, root_u = z // 2, root_z // 2
    z_is = [u == root_u ^ 1, u == second_of(root_u, 4), u == root_u ^ 2]
    early = [jnp.where(core == 0, a, b) for a, b in zip(x_is, z_is)]
    late = [jnp.where(core == 0, b, a) for a, b in zip(x_is, z_is)]
    is_root = at_y == 0
    for step, (zero, one) in enumerate(steps(parity)):
        swap = step in (1, 3)
        got1 = lax.ppermute(half_b if swap else half_a, ("row", "col"), places(*sizes, zero[0], one[0]))
        got2 = lax.ppermute(half_a if swap else half_b, ("row", "col"), places(*sizes, zero[1], one[1]))
        near, far, opposite = early if step < 2 else late
        if step == 0:
            upper_a, got1 = lax.optimization_barrier((upper_a, got1))
            up, down = shift(upper_a, 1), shift(upper_b, -1)
            upper_a, upper_b = jnp.where(at_y == 1, up, upper_a), jnp.where(at_y == 3, down, upper_b)
        if step == 1:
            upper_a, got1 = lax.optimization_barrier((upper_a, got1))
            up = shift(jnp.where(is_root, upper_b, upper_a), 1)
            down = shift(jnp.where(is_root, upper_a, upper_b), -1)
            upper_a = jnp.where(at_y == 2, up, jnp.where(at_y == 3, down, upper_a))
            upper_b = jnp.where(at_y == 1, up, jnp.where(at_y == 2, down, upper_b))
        if step == 3:
            upper_a, got1 = lax.optimization_barrier((upper_a, got1))
            other_a, other_b = cross(upper_a), cross(upper_b)
        if step == 4:
            other = z % 2 != parity
            half_a, half_b = jnp.where(other, got1, half_a), jnp.where(other, got2, half_b)
        elif swap:
            half_b = jnp.where(near | opposite, got1, half_b)
            half_a = jnp.where(far | opposite, got2, half_a)
        else:
            half_a = jnp.where(near, got1, half_a)
            half_b = jnp.where(far, got2, half_b)
    return half_a, half_b, upper_a, upper_b, other_a, other_b


def body(matrix, pattern, panel):
    grid_row, grid_col = lax.axis_index("row"), lax.axis_index("col")
    rows_here, cols_here = lax.axis_size("row"), lax.axis_size("col")
    block_rows, order, block_cols = matrix.shape[0], matrix.shape[2], matrix.shape[3]
    at = panel[0]
    local = matrix.reshape(block_rows, order, block_cols, order)
    core, y = grid_row % 2, grid_row // 2
    root_core, root_y = at % rows_here % 2, at % rows_here // 2
    tall = rows_here // 2
    at_y = (y - root_y + tall) % tall
    place = jnp.stack([core, jnp.int32(rows_here), jnp.int32(cols_here), grid_row, grid_col, at_y]).astype(jnp.int32)
    cross, shift = row_moves(rows_here)

    pivot, pivot_other = extract_pivot(local, panel, place)
    pivot = jnp.where(core == root_core, pivot, cross(pivot_other))

    info = plan_blocks(panel, pattern, place, pivot)
    up, down, over = shift(pivot, 1), shift(pivot, -1), shift(pivot, 2)
    base, left = mask_all(local, info)
    upper_a, upper_b, other_a, other_b, way = extract_upper(local, panel, place, left)
    from_a, from_b = cross(other_a), cross(other_b)
    way = way[0]
    pivot = jnp.where(way == 1, up, jnp.where(way == 3, down, jnp.where(way == 2, over, pivot)))
    pivot_other = cross(pivot)
    inverse, lower_a, lower_b = newton_lower(place, pivot, pivot_other, left)
    upper_a = jnp.where(core == root_core, upper_a, from_a)
    upper_b = jnp.where(core == root_core, upper_b, from_b)

    root = at % cols_here
    root_x, root_z = root // WIDE_Z, root % WIDE_Z
    *lower, upper_a, upper_b, other_a, other_b = lax.cond(
        root_z % 2 == 0,
        functools.partial(send_all, 0),
        functools.partial(send_all, 1),
        lower_a,
        lower_b,
        upper_a,
        upper_b,
        root_x,
        root_z,
        at_y,
    )
    result = update(base, info, lower, (upper_a, upper_b, other_a, other_b), inverse)
    return result.reshape(matrix.shape)


def solution(mesh):
    in_specs = (P(None, "row", None, None, "col", None), P(), P())
    out_specs = P(None, "row", None, None, "col", None)
    return jax.shard_map(body, mesh=mesh, in_specs=in_specs, out_specs=out_specs, check_vma=False)
```

```python
import functools

import jax
import jax.numpy as jnp
from jax import lax
from jax.experimental import pallas as pl
from jax.experimental.pallas import tpu as pltpu
from jax.sharding import PartitionSpec as P

SLOTS = 5
BLK = 256
HALF = 128
WIDE_Z = 8
MASK, SLOT, USED, ROWS, KEEP, HIT, CORE = 0, 32, 40, 48, 54, 58, 63


def first(t):
    return t ^ 1


def second(t, n):
    return (t + 1) % n if t % 2 else (t - 1) % n


def second_of(t, n):
    return jnp.where(t % 2 == 1, t + 1, t + n - 1) % n


def lanes(half):
    return slice(half * HALF, half * HALF + HALF)


def spread_rows(block, scratch):
    for half in range(2):
        scratch[:, half * 4 : half * 4 + 4, :] = block[:, :, lanes(half)].astype(jnp.float32)


def pivot_kernel(panel, place, block, mine, other, scratch):
    spread_rows(block[0], scratch)
    flat = scratch.reshape(BLK * 8, HALF)
    at = lax.div(panel[0], place[2])
    for half in range(2):
        for out, core in ((mine, place[0]), (other, 1 - place[0])):
            start = core * (HALF * 8) + half * 4 + at
            out[:, lanes(half)] = flat[pl.ds(start, HALF, stride=8), :].astype(jnp.bfloat16)


def extract_pivot(matrix, panel, place):
    half = jax.ShapeDtypeStruct((HALF, BLK), jnp.bfloat16)
    return pl.pallas_call(
        pivot_kernel,
        grid_spec=pltpu.PrefetchScalarGridSpec(
            num_scalar_prefetch=2,
            grid=(1,),
            in_specs=[pl.BlockSpec((1, BLK, 4, BLK), lambda s, panel, place: (lax.div(panel[0], place[1]), 0, 0, 0))],
            out_specs=[pl.BlockSpec((HALF, BLK), lambda s, *_: (0, 0))] * 2,
            scratch_shapes=[pltpu.VMEM((BLK, 8, HALF), jnp.float32)],
        ),
        out_shape=[half, half],
        name="extract_pivot",
    )(panel, place, matrix)


def upper_kernel(panel, place, block, after, mine_a, mine_b, other_a, other_b, scratch):
    spread_rows(block[0], scratch)
    flat = scratch.reshape(BLK * 8, HALF)
    core = place[0]
    for out, at in ((other_a, 2 - 2 * core), (other_b, 3 - 2 * core), (mine_a, 2 * core), (mine_b, 2 * core + 1)):
        for half in range(2):
            out[:, lanes(half)] = flat[pl.ds(half * 4 + at, BLK, stride=8), :].astype(jnp.bfloat16)


def extract_upper(matrix, panel, place, after):
    block = jax.ShapeDtypeStruct((BLK, BLK), jnp.bfloat16)
    return pl.pallas_call(
        upper_kernel,
        grid_spec=pltpu.PrefetchScalarGridSpec(
            num_scalar_prefetch=2,
            grid=(1,),
            in_specs=[pl.BlockSpec((1, BLK, 4, BLK), lambda s, panel, place: (lax.div(panel[0], place[1]), 0, 0, 0)), pl.BlockSpec(memory_space=pl.ANY)],
            out_specs=[pl.BlockSpec((BLK, BLK), lambda s, *_: (0, 0))] * 4,
            scratch_shapes=[pltpu.VMEM((BLK, 8, HALF), jnp.float32)],
        ),
        out_shape=[block] * 4,
        name="extract_upper",
    )(panel, place, matrix, after)


def plan_kernel(panel, pattern, place, after, info):
    at, rows, cols, grid_row, grid_col = panel[0], place[1], place[2], place[3], place[4]
    in_col = lax.rem(at, cols) == grid_col
    owner = in_col & (lax.rem(at, rows) == grid_row)
    used, reached, count = [], [], jnp.int32(0)
    for i in range(8):
        row = i * rows + grid_row
        here = ((pattern[row, at] != 0) & (row > at)).astype(jnp.int32)
        count = count + here
        used.append(here)
        reached.append(count)
        info[USED + i] = here
        info[SLOT + i] = jnp.maximum(count - 1, 0)
        for j in range(4):
            info[MASK + i * 4 + j] = pattern[row, j * cols + grid_col]
    for step in range(SLOTS + 1):
        wanted = jnp.minimum(max(step, 1), count)
        found = jnp.int32(0)
        for i in range(8):
            found = jnp.where((used[i] != 0) & (reached[i] == wanted), i, found)
        own = owner if step == 0 else owner & (count == 0)
        info[ROWS + step] = jnp.where(own, lax.div(at, rows), found)
    for j in range(4):
        column = j * cols + grid_col
        info[KEEP + j] = ((pattern[at, column] != 0) & (column > at)).astype(jnp.int32)
    info[HIT] = jnp.where(in_col, 1, -1)
    info[HIT + 1] = owner.astype(jnp.int32)
    info[HIT + 2] = lax.div(at, cols)
    info[HIT + 3] = lax.div(at - grid_row + rows - 1, rows)
    info[HIT + 4] = count
    info[CORE] = place[0]


def plan_blocks(panel, pattern, place, after):
    scalars = pl.BlockSpec(memory_space=pltpu.SMEM)
    return pl.pallas_call(
        plan_kernel,
        in_specs=[scalars] * 3 + [pl.BlockSpec(memory_space=pl.ANY)],
        out_specs=scalars,
        out_shape=jax.ShapeDtypeStruct((64,), jnp.int32),
        name="plan_blocks",
    )(panel, pattern, place, after)


def mask_kernel(info, block, out, panel):
    row = pl.program_id(0)
    column = lax.broadcasted_iota(jnp.int32, (BLK, 4, HALF), 1)
    on = jnp.zeros((BLK, 4, HALF), jnp.int32)
    for at in range(4):
        on = jnp.where(column == at, info[MASK + row * 4 + at], on)
    wide = out.reshape(BLK, 8, HALF)
    for half in range(2):
        piece = block[0, :, :, lanes(half)].astype(jnp.float32)
        wide[:, pl.ds(half, 4, stride=2), :] = jnp.where(on != 0, piece, 0.0)

    @pl.when(info[USED + row] != 0)
    def _():
        for half in range(2):
            panel[0, :, lanes(half)] = out[pl.ds(info[HIT + 2] * 2 + half, BLK, stride=8), :].astype(jnp.bfloat16)

    @pl.when((info[HIT] >= 0) & (row >= info[HIT + 3]))
    def _():
        for half in range(2):
            out[pl.ds(info[HIT + 2] * 2 + half, BLK, stride=8), :] = jnp.zeros((BLK, HALF), jnp.float32)


def mask_all(matrix, info):
    return pl.pallas_call(
        mask_kernel,
        grid_spec=pltpu.PrefetchScalarGridSpec(
            num_scalar_prefetch=1,
            grid=(8,),
            in_specs=[pl.BlockSpec((1, BLK, 4, BLK), lambda s, *_: (s, 0, 0, 0))],
            out_specs=[
                pl.BlockSpec((BLK * 8, HALF), lambda s, *_: (s, 0)),
                pl.BlockSpec((1, BLK, BLK), lambda s, info: (info[SLOT + s], 0, 0)),
            ],
        ),
        out_shape=[
            jax.ShapeDtypeStruct((8 * BLK * 8, HALF), jnp.float32),
            jax.ShapeDtypeStruct((SLOTS, BLK, BLK), jnp.bfloat16),
        ],
        name="mask_all",
        cost_estimate=pl.CostEstimate(flops=4 << 20, bytes_accessed=20 << 20, transcendentals=0),
        compiler_params=pltpu.CompilerParams(vmem_limit_bytes=24 * 1024 * 1024),
    )(info, matrix)


def halves(value):
    high = value.astype(jnp.bfloat16)
    return high, (value - high.astype(jnp.float32)).astype(jnp.bfloat16)


def product(left, right):
    (left_high, left_low), (right_high, right_low) = left, right
    dot = functools.partial(jnp.dot, preferred_element_type=jnp.float32)
    return dot(left_high, right_high) + (dot(left_high, right_low) + dot(left_low, right_high))


def newton_kernel(place, mine, other, panel, inverse, lower_a, lower_b):
    own, rest = mine[...].astype(jnp.float32), other[...].astype(jnp.float32)
    zero = place[0] == 0
    block = jnp.concatenate([jnp.where(zero, own, rest), jnp.where(zero, rest, own)], axis=0)
    down = lax.broadcasted_iota(jnp.int32, (BLK, BLK), 0)
    along = lax.broadcasted_iota(jnp.int32, (BLK, BLK), 1)
    same = down == along
    identity = jnp.where(same, 1.0, 0.0)
    diagonal = jnp.where(same, block, 0.0)
    error = identity - block * (1.0 / jnp.sum(diagonal, axis=0, keepdims=True))
    error_parts = halves(error)
    error2 = product(error_parts, error_parts)
    error2_parts = halves(error2)
    error4 = product(error2_parts, error2_parts)
    left = identity + error
    left = left + error2 + product(error_parts, error2_parts)
    left = left + product(halves(left), halves(error4))
    result = left * (1.0 / jnp.sum(diagonal, axis=1, keepdims=True))
    inverse[...] = result
    high, low = halves(result)
    for slot in range(SLOTS):
        rows = panel[slot]
        total = jnp.dot(rows, low, preferred_element_type=jnp.float32)
        total += jnp.dot(rows, high, preferred_element_type=jnp.float32)
        lower_a[slot] = total[:HALF].astype(jnp.bfloat16)
        lower_b[slot] = total[HALF:].astype(jnp.bfloat16)


def newton_lower(place, mine, other, panel):
    half = jax.ShapeDtypeStruct((SLOTS, HALF, BLK), jnp.bfloat16)
    return pl.pallas_call(
        newton_kernel,
        in_specs=[pl.BlockSpec(memory_space=pltpu.SMEM)] + [pl.BlockSpec(memory_space=pltpu.VMEM)] * 3,
        out_shape=[jax.ShapeDtypeStruct((BLK, BLK), jnp.float32), half, half],
        name="newton_lower",
    )(place, mine, other, panel)


def update_kernel(info, base, lower_a, lower_b, mine_a, mine_b, other_a, other_b, inverse, out):
    step = pl.program_id(0)
    row = info[ROWS + step]
    before = info[ROWS + jnp.maximum(step - 1, 0)]

    @pl.when((step == 0) | (row != before))
    def _():
        out[...] = base[...]

    live = (step > 0) & (step <= info[HIT + 4])
    slot = jnp.maximum(step - 1, 0)
    core = info[CORE]
    for at in range(4):
        own, others = ((mine_a, other_a), (mine_b, other_b))[at % 2]

        @pl.when(live & (info[KEEP + at] != 0))
        def _():
            right = jnp.where(core == at // 2, own[...], others[...])
            left = jnp.concatenate([lower_a[slot], lower_b[slot]], axis=0)
            change = jnp.dot(left, right, preferred_element_type=jnp.float32)
            for half in range(2):
                into = pl.ds(at * 2 + half, BLK, stride=8)
                out[into, :] = base[into, :] - change[:, lanes(half)]

    @pl.when(live & (info[HIT] >= 0))
    def _():
        for part, lower in enumerate((lower_a, lower_b)):
            for half in range(2):
                into = pl.ds(part * HALF * 8 + info[HIT + 2] * 2 + half, HALF, stride=8)
                out[into, :] = lower[slot, :, lanes(half)].astype(jnp.float32)

    @pl.when((step == 0) & (info[HIT + 1] != 0))
    def _():
        for half in range(2):
            out[pl.ds(info[HIT + 2] * 2 + half, BLK, stride=8), :] = inverse[:, lanes(half)]


def update(base, info, lower, upper, inverse):
    whole = lambda *shape: pl.BlockSpec(shape, lambda s, *_: (0,) * len(shape))
    return pl.pallas_call(
        update_kernel,
        grid_spec=pltpu.PrefetchScalarGridSpec(
            num_scalar_prefetch=1,
            grid=(SLOTS + 1,),
            in_specs=[pl.BlockSpec((BLK * 8, HALF), lambda s, info: (info[ROWS + s], 0))]
            + [whole(SLOTS, HALF, BLK)] * 2
            + [whole(BLK, BLK)] * 5,
            out_specs=pl.BlockSpec((BLK * 8, HALF), lambda s, info: (info[ROWS + s], 0)),
        ),
        out_shape=jax.ShapeDtypeStruct(base.shape, jnp.float32),
        input_output_aliases={1: 0},
        name="update",
        compiler_params=pltpu.CompilerParams(vmem_limit_bytes=24 * 1024 * 1024),
    )(info, base, *lower, *upper, inverse)


def places(size_row, size_col, core_zero, core_one):
    pairs = []
    for row in range(size_row):
        for at in range(size_col):
            to = (core_one if row % 2 else core_zero)(at // 8, at % 8)
            if to is not None:
                pairs.append((row * size_col + at, row * size_col + to[0] * 8 + to[1]))
    return pairs


def steps(parity):
    x1 = lambda x, z: (first(x), z)
    x2 = lambda x, z: (second(x, 4), z)
    mine = lambda z: z % 2 == parity
    z1 = lambda x, z: (x, first(z // 2) * 2 + parity) if mine(z) else None
    z2 = lambda x, z: (x, second(z // 2, 4) * 2 + parity) if mine(z) else None
    n1 = lambda x, z: (x, first(z))
    n2 = lambda x, z: (x, second(z, 8))
    across, along, last = (x1, x2), (z1, z2), (n1, n2)
    return [(across, along), (across, along), (along, across), (along, across), (last, last)]


def row_moves(rows):
    flip = [(r, r ^ 1) for r in range(rows)]
    shift = lambda value, by: lax.ppermute(value, "row", [(r, (r + 2 * by) % rows) for r in range(rows)])
    return lambda value: lax.ppermute(value, "row", flip), shift


def send_all(parity, half_a, half_b, upper_a, upper_b, root_x, root_z, at_y):
    row, col = lax.axis_index("row"), lax.axis_index("col")
    sizes = lax.axis_size("row"), lax.axis_size("col")
    cross, shift = row_moves(sizes[0])
    core, x, z = row % 2, col // WIDE_Z, col % WIDE_Z
    x_is = [x == root_x ^ 1, x == second_of(root_x, 4), x == root_x ^ 2]
    u, root_u = z // 2, root_z // 2
    z_is = [u == root_u ^ 1, u == second_of(root_u, 4), u == root_u ^ 2]
    early = [jnp.where(core == 0, a, b) for a, b in zip(x_is, z_is)]
    late = [jnp.where(core == 0, b, a) for a, b in zip(x_is, z_is)]
    is_root = at_y == 0
    for step, (zero, one) in enumerate(steps(parity)):
        swap = step in (1, 3)
        got1 = lax.ppermute(half_b if swap else half_a, ("row", "col"), places(*sizes, zero[0], one[0]))
        got2 = lax.ppermute(half_a if swap else half_b, ("row", "col"), places(*sizes, zero[1], one[1]))
        near, far, opposite = early if step < 2 else late
        if step == 0:
            upper_a, got1 = lax.optimization_barrier((upper_a, got1))
            up, down = shift(upper_a, 1), shift(upper_b, -1)
            upper_a, upper_b = jnp.where(at_y == 1, up, upper_a), jnp.where(at_y == 3, down, upper_b)
        if step == 1:
            upper_a, got1 = lax.optimization_barrier((upper_a, got1))
            up = shift(jnp.where(is_root, upper_b, upper_a), 1)
            down = shift(jnp.where(is_root, upper_a, upper_b), -1)
            upper_a = jnp.where(at_y == 2, up, jnp.where(at_y == 3, down, upper_a))
            upper_b = jnp.where(at_y == 1, up, jnp.where(at_y == 2, down, upper_b))
        if step == 3:
            upper_a, got1 = lax.optimization_barrier((upper_a, got1))
            other_a, other_b = cross(upper_a), cross(upper_b)
        if step == 4:
            other = z % 2 != parity
            half_a, half_b = jnp.where(other, got1, half_a), jnp.where(other, got2, half_b)
        elif swap:
            half_b = jnp.where(near | opposite, got1, half_b)
            half_a = jnp.where(far | opposite, got2, half_a)
        else:
            half_a = jnp.where(near, got1, half_a)
            half_b = jnp.where(far, got2, half_b)
    return half_a, half_b, upper_a, upper_b, other_a, other_b


def body(matrix, pattern, panel):
    grid_row, grid_col = lax.axis_index("row"), lax.axis_index("col")
    rows_here, cols_here = lax.axis_size("row"), lax.axis_size("col")
    block_rows, order, block_cols = matrix.shape[0], matrix.shape[2], matrix.shape[3]
    at = panel[0]
    local = matrix.reshape(block_rows, order, block_cols, order)
    core, y = grid_row % 2, grid_row // 2
    root_core, root_y = at % rows_here % 2, at % rows_here // 2
    tall = rows_here // 2
    at_y = (y - root_y + tall) % tall
    place = jnp.stack([core, jnp.int32(rows_here), jnp.int32(cols_here), grid_row, grid_col]).astype(jnp.int32)
    cross, shift = row_moves(rows_here)

    pivot, pivot_other = extract_pivot(local, panel, place)
    pivot = jnp.where(core == root_core, pivot, cross(pivot_other))

    info = plan_blocks(panel, pattern, place, pivot)
    up, down, over = shift(pivot, 1), shift(pivot, -1), shift(pivot, 2)
    base, left = mask_all(local, info)
    upper_a, upper_b, other_a, other_b = extract_upper(local, panel, place, left)
    from_a, from_b = cross(other_a), cross(other_b)
    pivot = jnp.where(at_y == 1, up, jnp.where(at_y == 3, down, jnp.where(at_y == 2, over, pivot)))
    pivot_other = cross(pivot)
    inverse, lower_a, lower_b = newton_lower(place, pivot, pivot_other, left)
    upper_a = jnp.where(core == root_core, upper_a, from_a)
    upper_b = jnp.where(core == root_core, upper_b, from_b)

    root = at % cols_here
    root_x, root_z = root // WIDE_Z, root % WIDE_Z
    *lower, upper_a, upper_b, other_a, other_b = lax.cond(
        root_z % 2 == 0,
        functools.partial(send_all, 0),
        functools.partial(send_all, 1),
        lower_a,
        lower_b,
        upper_a,
        upper_b,
        root_x,
        root_z,
        at_y,
    )
    result = update(base, info, lower, (upper_a, upper_b, other_a, other_b), inverse)
    return result.reshape(matrix.shape)


def solution(mesh):
    in_specs = (P(None, "row", None, None, "col", None), P(), P())
    out_specs = P(None, "row", None, None, "col", None)
    return jax.shard_map(body, mesh=mesh, in_specs=in_specs, out_specs=out_specs, check_vma=False)
```

```python
import functools

import jax
import jax.numpy as jnp
from jax import lax
from jax.experimental import pallas as pl
from jax.experimental.pallas import tpu as pltpu
from jax.sharding import PartitionSpec as P

SLOTS = 5
BLK = 256
HALF = 128
WIDE_Z = 8
MASK, SLOT, USED, ROWS, KEEP, HIT, CORE = 0, 32, 40, 48, 54, 58, 63


def first(t):
    return t ^ 1


def second(t, n):
    return (t + 1) % n if t % 2 else (t - 1) % n


def second_of(t, n):
    return jnp.where(t % 2 == 1, t + 1, t + n - 1) % n


def lanes(half):
    return slice(half * HALF, half * HALF + HALF)


def spread_rows(block, scratch):
    for half in range(2):
        scratch[:, half * 4 : half * 4 + 4, :] = block[:, :, lanes(half)].astype(jnp.float32)


def pivot_kernel(panel, place, block, mine, other, scratch):
    spread_rows(block[0], scratch)
    flat = scratch.reshape(BLK * 8, HALF)
    at = lax.div(panel[0], place[2])
    for half in range(2):
        for out, core in ((mine, place[0]), (other, 1 - place[0])):
            start = core * (HALF * 8) + half * 4 + at
            out[:, lanes(half)] = flat[pl.ds(start, HALF, stride=8), :].astype(jnp.bfloat16)


def extract_pivot(matrix, panel, place):
    half = jax.ShapeDtypeStruct((HALF, BLK), jnp.bfloat16)
    return pl.pallas_call(
        pivot_kernel,
        grid_spec=pltpu.PrefetchScalarGridSpec(
            num_scalar_prefetch=2,
            grid=(1,),
            in_specs=[pl.BlockSpec((1, BLK, 4, BLK), lambda s, panel, place: (lax.div(panel[0], place[1]), 0, 0, 0))],
            out_specs=[pl.BlockSpec((HALF, BLK), lambda s, *_: (0, 0))] * 2,
            scratch_shapes=[pltpu.VMEM((BLK, 8, HALF), jnp.float32)],
        ),
        out_shape=[half, half],
        name="extract_pivot",
    )(panel, place, matrix)


def upper_kernel(panel, place, block, after, mine_a, mine_b, other_a, other_b, scratch):
    spread_rows(block[0], scratch)
    flat = scratch.reshape(BLK * 8, HALF)
    core = place[0]
    for out, at in ((other_a, 2 - 2 * core), (other_b, 3 - 2 * core), (mine_a, 2 * core), (mine_b, 2 * core + 1)):
        for half in range(2):
            out[:, lanes(half)] = flat[pl.ds(half * 4 + at, BLK, stride=8), :].astype(jnp.bfloat16)


def extract_upper(matrix, panel, place, after):
    block = jax.ShapeDtypeStruct((BLK, BLK), jnp.bfloat16)
    return pl.pallas_call(
        upper_kernel,
        grid_spec=pltpu.PrefetchScalarGridSpec(
            num_scalar_prefetch=2,
            grid=(1,),
            in_specs=[pl.BlockSpec((1, BLK, 4, BLK), lambda s, panel, place: (lax.div(panel[0], place[1]), 0, 0, 0)), pl.BlockSpec(memory_space=pl.ANY)],
            out_specs=[pl.BlockSpec((BLK, BLK), lambda s, *_: (0, 0))] * 4,
            scratch_shapes=[pltpu.VMEM((BLK, 8, HALF), jnp.float32)],
        ),
        out_shape=[block] * 4,
        name="extract_upper",
    )(panel, place, matrix, after)


def plan_kernel(panel, pattern, place, after, info):
    at, rows, cols, grid_row, grid_col = panel[0], place[1], place[2], place[3], place[4]
    in_col = lax.rem(at, cols) == grid_col
    owner = in_col & (lax.rem(at, rows) == grid_row)
    used, reached, count = [], [], jnp.int32(0)
    for i in range(8):
        row = i * rows + grid_row
        here = ((pattern[row, at] != 0) & (row > at)).astype(jnp.int32)
        count = count + here
        used.append(here)
        reached.append(count)
        info[USED + i] = here
        info[SLOT + i] = jnp.maximum(count - 1, 0)
        for j in range(4):
            info[MASK + i * 4 + j] = pattern[row, j * cols + grid_col]
    for step in range(SLOTS + 1):
        wanted = jnp.minimum(max(step, 1), count)
        found = jnp.int32(0)
        for i in range(8):
            found = jnp.where((used[i] != 0) & (reached[i] == wanted), i, found)
        own = owner if step == 0 else owner & (count == 0)
        info[ROWS + step] = jnp.where(own, lax.div(at, rows), found)
    for j in range(4):
        column = j * cols + grid_col
        info[KEEP + j] = ((pattern[at, column] != 0) & (column > at)).astype(jnp.int32)
    info[HIT] = jnp.where(in_col, 1, -1)
    info[HIT + 1] = owner.astype(jnp.int32)
    info[HIT + 2] = lax.div(at, cols)
    info[HIT + 3] = lax.div(at - grid_row + rows - 1, rows)
    info[HIT + 4] = count
    info[CORE] = place[0]


def plan_blocks(panel, pattern, place, after):
    scalars = pl.BlockSpec(memory_space=pltpu.SMEM)
    return pl.pallas_call(
        plan_kernel,
        in_specs=[scalars] * 3 + [pl.BlockSpec(memory_space=pl.ANY)],
        out_specs=scalars,
        out_shape=jax.ShapeDtypeStruct((64,), jnp.int32),
        name="plan_blocks",
    )(panel, pattern, place, after)


def mask_kernel(info, block, out, panel):
    row = pl.program_id(0)
    column = lax.broadcasted_iota(jnp.int32, (BLK, 4, HALF), 1)
    on = jnp.zeros((BLK, 4, HALF), jnp.int32)
    for at in range(4):
        on = jnp.where(column == at, info[MASK + row * 4 + at], on)
    wide = out.reshape(BLK, 8, HALF)
    for half in range(2):
        piece = block[0, :, :, lanes(half)].astype(jnp.float32)
        wide[:, pl.ds(half, 4, stride=2), :] = jnp.where(on != 0, piece, 0.0)

    @pl.when(info[USED + row] != 0)
    def _():
        for half in range(2):
            panel[0, :, lanes(half)] = out[pl.ds(info[HIT + 2] * 2 + half, BLK, stride=8), :].astype(jnp.bfloat16)

    @pl.when((info[HIT] >= 0) & (row >= info[HIT + 3]))
    def _():
        for half in range(2):
            out[pl.ds(info[HIT + 2] * 2 + half, BLK, stride=8), :] = jnp.zeros((BLK, HALF), jnp.float32)


def mask_all(matrix, info):
    return pl.pallas_call(
        mask_kernel,
        grid_spec=pltpu.PrefetchScalarGridSpec(
            num_scalar_prefetch=1,
            grid=(8,),
            in_specs=[pl.BlockSpec((1, BLK, 4, BLK), lambda s, *_: (s, 0, 0, 0))],
            out_specs=[
                pl.BlockSpec((BLK * 8, HALF), lambda s, *_: (s, 0)),
                pl.BlockSpec((1, BLK, BLK), lambda s, info: (info[SLOT + s], 0, 0)),
            ],
        ),
        out_shape=[
            jax.ShapeDtypeStruct((8 * BLK * 8, HALF), jnp.float32),
            jax.ShapeDtypeStruct((SLOTS, BLK, BLK), jnp.bfloat16),
        ],
        name="mask_all",
        cost_estimate=pl.CostEstimate(flops=4 << 20, bytes_accessed=20 << 20, transcendentals=0),
        compiler_params=pltpu.CompilerParams(vmem_limit_bytes=24 * 1024 * 1024),
    )(info, matrix)


def halves(value):
    high = value.astype(jnp.bfloat16)
    return high, (value - high.astype(jnp.float32)).astype(jnp.bfloat16)


def product(left, right):
    (left_high, left_low), (right_high, right_low) = left, right
    dot = functools.partial(jnp.dot, preferred_element_type=jnp.float32)
    return dot(left_high, right_high) + (dot(left_high, right_low) + dot(left_low, right_high))


def newton_kernel(place, mine, other, panel, inverse, lower_a, lower_b):
    own, rest = mine[...].astype(jnp.float32), other[...].astype(jnp.float32)
    zero = place[0] == 0
    block = jnp.concatenate([jnp.where(zero, own, rest), jnp.where(zero, rest, own)], axis=0)
    down = lax.broadcasted_iota(jnp.int32, (BLK, BLK), 0)
    along = lax.broadcasted_iota(jnp.int32, (BLK, BLK), 1)
    same = down == along
    identity = jnp.where(same, 1.0, 0.0)
    diagonal = jnp.where(same, block, 0.0)
    error = identity - block * (1.0 / jnp.sum(diagonal, axis=0, keepdims=True))
    error_parts = halves(error)
    error2 = product(error_parts, error_parts)
    error2_parts = halves(error2)
    error4 = product(error2_parts, error2_parts)
    left = identity + error
    left = left + error2 + product(error_parts, error2_parts)
    left = left + product(halves(left), halves(error4))
    result = left * (1.0 / jnp.sum(diagonal, axis=1, keepdims=True))
    inverse[...] = result
    high, low = halves(result)
    for slot in range(SLOTS):
        rows = panel[slot]
        total = jnp.dot(rows, low, preferred_element_type=jnp.float32)
        total += jnp.dot(rows, high, preferred_element_type=jnp.float32)
        lower_a[slot] = total[:HALF].astype(jnp.bfloat16)
        lower_b[slot] = total[HALF:].astype(jnp.bfloat16)


def newton_lower(place, mine, other, panel):
    half = jax.ShapeDtypeStruct((SLOTS, HALF, BLK), jnp.bfloat16)
    return pl.pallas_call(
        newton_kernel,
        in_specs=[pl.BlockSpec(memory_space=pltpu.SMEM)] + [pl.BlockSpec(memory_space=pltpu.VMEM)] * 3,
        out_shape=[jax.ShapeDtypeStruct((BLK, BLK), jnp.float32), half, half],
        name="newton_lower",
    )(place, mine, other, panel)


def update_kernel(info, base, lower_a, lower_b, mine_a, mine_b, other_a, other_b, inverse, out):
    step = pl.program_id(0)
    row = info[ROWS + step]
    before = info[ROWS + jnp.maximum(step - 1, 0)]

    @pl.when((step == 0) | (row != before))
    def _():
        out[...] = base[...]

    live = (step > 0) & (step <= info[HIT + 4])
    slot = jnp.maximum(step - 1, 0)
    core = info[CORE]
    for at in range(4):
        own, others = ((mine_a, other_a), (mine_b, other_b))[at % 2]

        @pl.when(live & (info[KEEP + at] != 0))
        def _():
            right = jnp.where(core == at // 2, own[...], others[...])
            left = jnp.concatenate([lower_a[slot], lower_b[slot]], axis=0)
            change = jnp.dot(left, right, preferred_element_type=jnp.float32)
            for half in range(2):
                into = pl.ds(at * 2 + half, BLK, stride=8)
                out[into, :] = base[into, :] - change[:, lanes(half)]

    @pl.when(live & (info[HIT] >= 0))
    def _():
        for part, lower in enumerate((lower_a, lower_b)):
            for half in range(2):
                into = pl.ds(part * HALF * 8 + info[HIT + 2] * 2 + half, HALF, stride=8)
                out[into, :] = lower[slot, :, lanes(half)].astype(jnp.float32)

    @pl.when((step == 0) & (info[HIT + 1] != 0))
    def _():
        for half in range(2):
            out[pl.ds(info[HIT + 2] * 2 + half, BLK, stride=8), :] = inverse[:, lanes(half)]


def update(base, info, lower, upper, inverse):
    whole = lambda *shape: pl.BlockSpec(shape, lambda s, *_: (0,) * len(shape))
    return pl.pallas_call(
        update_kernel,
        grid_spec=pltpu.PrefetchScalarGridSpec(
            num_scalar_prefetch=1,
            grid=(SLOTS + 1,),
            in_specs=[pl.BlockSpec((BLK * 8, HALF), lambda s, info: (info[ROWS + s], 0))]
            + [whole(SLOTS, HALF, BLK)] * 2
            + [whole(BLK, BLK)] * 5,
            out_specs=pl.BlockSpec((BLK * 8, HALF), lambda s, info: (info[ROWS + s], 0)),
        ),
        out_shape=jax.ShapeDtypeStruct(base.shape, jnp.float32),
        input_output_aliases={1: 0},
        name="update",
        compiler_params=pltpu.CompilerParams(vmem_limit_bytes=24 * 1024 * 1024),
    )(info, base, *lower, *upper, inverse)


def places(size_row, size_col, core_zero, core_one):
    pairs = []
    for row in range(size_row):
        for at in range(size_col):
            to = (core_one if row % 2 else core_zero)(at // 8, at % 8)
            if to is not None:
                pairs.append((row * size_col + at, row * size_col + to[0] * 8 + to[1]))
    return pairs


def steps(parity):
    mine = lambda z: z % 2 == parity
    x1 = lambda x, z: (first(x), z) if mine(z) else None
    x2 = lambda x, z: (second(x, 4), z) if mine(z) else None
    z1 = lambda x, z: (x, first(z // 2) * 2 + parity) if mine(z) else None
    z2 = lambda x, z: (x, second(z // 2, 4) * 2 + parity) if mine(z) else None
    up = lambda x, z: (x, (z + 1) % WIDE_Z) if mine(z) else None
    down = lambda x, z: (x, (z - 1) % WIDE_Z) if mine(z) else None
    across, along, last = (x1, x2), (z1, z2), (up, down)
    return [(across, along), (across, along), (along, across), (along, across), (last, last)]


def row_moves(rows):
    flip = [(r, r ^ 1) for r in range(rows)]
    shift = lambda value, by: lax.ppermute(value, "row", [(r, (r + 2 * by) % rows) for r in range(rows)])
    return lambda value: lax.ppermute(value, "row", flip), shift


def send_all(parity, half_a, half_b, upper_a, upper_b, root_x, root_z, at_y):
    row, col = lax.axis_index("row"), lax.axis_index("col")
    sizes = lax.axis_size("row"), lax.axis_size("col")
    cross, shift = row_moves(sizes[0])
    core, x, z = row % 2, col // WIDE_Z, col % WIDE_Z
    x_is = [x == root_x ^ 1, x == second_of(root_x, 4), x == root_x ^ 2]
    u, root_u = z // 2, root_z // 2
    z_is = [u == root_u ^ 1, u == second_of(root_u, 4), u == root_u ^ 2]
    early = [jnp.where(core == 0, a, b) for a, b in zip(x_is, z_is)]
    late = [jnp.where(core == 0, b, a) for a, b in zip(x_is, z_is)]
    is_root = at_y == 0
    for step, (zero, one) in enumerate(steps(parity)):
        swap = step in (1, 3)
        got1 = lax.ppermute(half_b if swap else half_a, ("row", "col"), places(*sizes, zero[0], one[0]))
        got2 = lax.ppermute(half_a if swap else half_b, ("row", "col"), places(*sizes, zero[1], one[1]))
        near, far, opposite = early if step < 2 else late
        if step == 0:
            upper_a, got1 = lax.optimization_barrier((upper_a, got1))
            up, down = shift(upper_a, 1), shift(upper_b, -1)
            upper_a, upper_b = jnp.where(at_y == 1, up, upper_a), jnp.where(at_y == 3, down, upper_b)
        if step == 1:
            upper_a, got1 = lax.optimization_barrier((upper_a, got1))
            up = shift(jnp.where(is_root, upper_b, upper_a), 1)
            down = shift(jnp.where(is_root, upper_a, upper_b), -1)
            upper_a = jnp.where(at_y == 2, up, jnp.where(at_y == 3, down, upper_a))
            upper_b = jnp.where(at_y == 1, up, jnp.where(at_y == 2, down, upper_b))
        if step == 3:
            upper_a, got1 = lax.optimization_barrier((upper_a, got1))
            other_a, other_b = cross(upper_a), cross(upper_b)
        if step == 4:
            other = z % 2 != parity
            half_a, half_b = jnp.where(other, got1, half_a), jnp.where(other, got2, half_b)
        elif swap:
            half_b = jnp.where(near | opposite, got1, half_b)
            half_a = jnp.where(far | opposite, got2, half_a)
        else:
            half_a = jnp.where(near, got1, half_a)
            half_b = jnp.where(far, got2, half_b)
    return half_a, half_b, upper_a, upper_b, other_a, other_b


def body(matrix, pattern, panel):
    grid_row, grid_col = lax.axis_index("row"), lax.axis_index("col")
    rows_here, cols_here = lax.axis_size("row"), lax.axis_size("col")
    block_rows, order, block_cols = matrix.shape[0], matrix.shape[2], matrix.shape[3]
    at = panel[0]
    local = matrix.reshape(block_rows, order, block_cols, order)
    core, y = grid_row % 2, grid_row // 2
    root_core, root_y = at % rows_here % 2, at % rows_here // 2
    tall = rows_here // 2
    at_y = (y - root_y + tall) % tall
    place = jnp.stack([core, jnp.int32(rows_here), jnp.int32(cols_here), grid_row, grid_col]).astype(jnp.int32)
    cross, shift = row_moves(rows_here)

    pivot, pivot_other = extract_pivot(local, panel, place)
    pivot = jnp.where(core == root_core, pivot, cross(pivot_other))

    info = plan_blocks(panel, pattern, place, pivot)
    up, down, over = shift(pivot, 1), shift(pivot, -1), shift(pivot, 2)
    base, left = mask_all(local, info)
    upper_a, upper_b, other_a, other_b = extract_upper(local, panel, place, left)
    from_a, from_b = cross(other_a), cross(other_b)
    pivot = jnp.where(at_y == 1, up, jnp.where(at_y == 3, down, jnp.where(at_y == 2, over, pivot)))
    pivot_other = cross(pivot)
    inverse, lower_a, lower_b = newton_lower(place, pivot, pivot_other, left)
    upper_a = jnp.where(core == root_core, upper_a, from_a)
    upper_b = jnp.where(core == root_core, upper_b, from_b)

    root = at % cols_here
    root_x, root_z = root // WIDE_Z, root % WIDE_Z
    *lower, upper_a, upper_b, other_a, other_b = lax.cond(
        root_z % 2 == 0,
        functools.partial(send_all, 0),
        functools.partial(send_all, 1),
        lower_a,
        lower_b,
        upper_a,
        upper_b,
        root_x,
        root_z,
        at_y,
    )
    result = update(base, info, lower, (upper_a, upper_b, other_a, other_b), inverse)
    return result.reshape(matrix.shape)


def solution(mesh):
    in_specs = (P(None, "row", None, None, "col", None), P(), P())
    out_specs = P(None, "row", None, None, "col", None)
    return jax.shard_map(body, mesh=mesh, in_specs=in_specs, out_specs=out_specs, check_vma=False)
```
